512 devices in a mesh: ctx: 64 (over z, x), head: 8 (over y, core).
Axes of the slice: x: 4, y: 4, z: 16, core: 2. Of those that a mesh axis runs over, the one named last changes fastest.
Arguments:
- inputs: bfloat16 [16384, 2048], P('ctx', 'head'), may hold values from -16 to 16
- w_query: bfloat16 [2048, 2048], P(None, 'head'), may hold values from -0.125 to 0.125
- w_key: bfloat16 [2048, 2048], P(None, 'head'), may hold values from -0.125 to 0.125
- w_value: bfloat16 [2048, 2048], P(None, 'head'), may hold values from -0.125 to 0.125
- w_out: bfloat16 [2048, 2048], P('head'), may hold values from -0.125 to 0.125
- reflect_dir: bfloat16 [16384, 2048], P('ctx', 'head'), may hold values from -25 to 25
- strength: float32 [16, 16384], P('head', 'ctx'), may hold values from 0.5 to 1.5
- hop_count: int32 [64], P('ctx'), may hold values from 1 to 8, as said below
Outputs:
- mixed: bfloat16 [16384, 2048], P('ctx', 'head')
The draws below stay inside these ranges and needn't reach their ends.
Inputs may be any that keep to these rules, and one draw needn't show every extreme that they name: `hop_count`: some block has exactly 8.
All inputs are finite; a program needn't handle non-finite values.
Results may differ from the reference program's by a relative error of at most 0.019.
Values may be sent and summed in bfloat16 or wider, within the bound.
No kernel may reach another device: no remote copies, remote signals or barrier semaphores. Data moves between devices by JAX's collectives and lax.ppermute only.
A program may use at most 64 MiB of HBM per device.

```python
import jax
import jax.numpy as jnp
from jax import lax

D = 2048
H = 16
DH = 128
TOK = 256
HOPS = 8
SHARDS = 64
TOKENS = 16384


def draw_inputs(key, part):
    key = jax.random.fold_in(key, 11)
    first = jax.random.fold_in(key, 0)
    return jnp.clip(jax.random.normal(first, (TOKENS, D), jnp.float32), -6.0, 6.0).astype(jnp.bfloat16)


def draw_reflect_dir(key, part):
    key = jax.random.fold_in(key, 23)
    first, second = jax.random.split(key)
    gains = jnp.exp(jax.random.uniform(first, (1, H * DH), jnp.float32, -2.0, 1.4))
    base = jnp.clip(jax.random.normal(second, (TOKENS, H * DH), jnp.float32), -6.0, 6.0)
    return (base * gains).astype(jnp.bfloat16)


def draw_hop_count(key, part):
    key = jax.random.fold_in(key, 37)
    first, second = jax.random.split(key)
    counts = jax.random.randint(first, (SHARDS,), 1, HOPS + 1, dtype=jnp.int32)
    marked = jax.random.randint(second, (), 0, SHARDS, dtype=jnp.int32)
    blocks = jnp.arange(SHARDS, dtype=jnp.int32)
    return jnp.where(blocks == marked, jnp.int32(HOPS), counts).astype(jnp.int32)


def steps_of(own_key, dims, pieces, least, largest):
    level = 1.0
    for position, shards_of in pieces:
        draws = jax.random.uniform(jax.random.fold_in(jax.random.fold_in(own_key, 6), position), (shards_of,), jnp.float32, least / len(pieces), largest / len(pieces))
        level = level * jnp.repeat(jnp.exp(draws), dims[position] // shards_of).reshape((-1,) + (1,) * (len(dims) - 1 - position))
    return level


def normal_values(stream_key, shape, deviation, most, pieces=(), kind=jnp.bfloat16):
    result = deviation * jax.random.normal(stream_key, shape, jnp.float32)
    if pieces:
        result = result * steps_of(stream_key, shape, pieces, -0.22, 0.18)
    return jnp.clip(result, -most, most).astype(kind)


def setup_inputs(seed: int = 0) -> dict:
    splits = jax.random.split(jax.random.key(seed), 9)
    inputs = draw_inputs(jax.random.fold_in(splits[8], 71), 0)
    w_query = normal_values(splits[1], (D, H * DH), D ** -0.5, 0.125, ((1, 8),))
    w_key = normal_values(splits[2], (D, H * DH), D ** -0.5, 0.125, ((1, 8),))
    w_value = normal_values(splits[3], (D, H * DH), D ** -0.5, 0.125, ((1, 8),))
    w_out = normal_values(splits[4], (H * DH, D), (H * DH) ** -0.5, 0.125, ((0, 8),))
    reflect_dir = draw_reflect_dir(jax.random.fold_in(splits[8], 71), 0)
    strength = jnp.clip(0.5 + 1.0 * jax.random.uniform(splits[6], (H, TOKENS), jnp.float32) ** steps_of(splits[6], (H, TOKENS), ((0, 8), (1, 64)), -0.2, 0.2), 0.5, 1.5)
    hop_count = draw_hop_count(jax.random.fold_in(splits[8], 71), 0)
    return {"inputs": inputs, "w_query": w_query, "w_key": w_key, "w_value": w_value, "w_out": w_out, "reflect_dir": reflect_dir, "strength": strength, "hop_count": hop_count}


def heads_first(array):
    return array.reshape(SHARDS, TOK, H, DH).transpose(2, 0, 1, 3)

def single_head(operands):
    qh, kh, vh, dirs, beta, count = operands
    upper_bound = lax.Precision.HIGHEST
    scale = 1.0 / DH ** 0.5
    positions = jnp.arange(TOK, dtype=jnp.int32)

    def advance(carry, item):
        present_keys, product = carry
        step, query_row, krow, weight_row, brow = item
        walk_through = jnp.einsum('hpr,hr->hp', present_keys, weight_row, precision=upper_bound)
        present_keys = present_keys - brow[:, None, None] * walk_through[:, :, None] * weight_row[:, None, :]
        placed = (positions == step).astype(jnp.float32)
        present_keys = present_keys + placed[None, :, None] * krow[:, None, :]
        score_row_values = jnp.einsum('hpr,hr->hp', present_keys, query_row, precision=upper_bound)
        across = jnp.einsum('sd,sde->se', weight_row, product, precision=upper_bound)
        product = product - brow[:, None, None] * weight_row[:, :, None] * across[:, None, :]
        moved = jnp.einsum('sde,sd->se', product, query_row, precision=upper_bound)
        return ((present_keys, product), (score_row_values, moved))
    init = (jnp.zeros((SHARDS, TOK, DH), jnp.float32), jnp.broadcast_to(jnp.eye(DH, dtype=jnp.float32), (SHARDS, DH, DH)))
    items = (positions, qh.transpose(1, 0, 2), kh.transpose(1, 0, 2), dirs.transpose(1, 0, 2), beta.transpose(1, 0))
    (khat, trans), (rows, moved) = lax.scan(advance, init, items)
    own = rows.transpose(1, 0, 2) * scale
    lower = positions[:, None] >= positions[None, :]
    own = jnp.where(lower[None], own, -jnp.inf)
    qhat = moved.transpose(1, 0, 2)
    blocks = jnp.arange(SHARDS, dtype=jnp.int32)
    all_scores = [own]
    all_values = [vh]
    current = khat
    carried = vh
    for hop in range(1, HOPS + 1):
        current = jnp.concatenate([jnp.zeros_like(current[:1]), current[:-1]], axis=0)
        carried = jnp.concatenate([jnp.zeros_like(carried[:1]), carried[:-1]], axis=0)
        block_scores = jnp.einsum('sqd,skd->sqk', qhat, current, precision=upper_bound) * scale
        valid = (hop <= count) & (blocks >= hop)
        all_scores.append(jnp.where(valid[:, None, None], block_scores, -jnp.inf))
        all_values.append(carried)
        current = jnp.einsum('sed,skd->ske', trans, current, precision=upper_bound)
    scores = jnp.concatenate(all_scores, axis=2)
    values = jnp.concatenate(all_values, axis=1)
    top = lax.optimization_barrier(jnp.max(scores, axis=2, keepdims=True))
    prob = jnp.exp(scores - top)
    total = lax.optimization_barrier(jnp.sum(prob, axis=2, keepdims=True))
    weights = prob.astype(jnp.bfloat16).astype(jnp.float32)
    summed = jnp.einsum('sqk,skd->sqd', weights, values.astype(jnp.float32))
    return (summed / total).astype(jnp.bfloat16)

def reference(inputs, w_query, w_key, w_value, w_out, reflect_dir, strength, hop_count):
    query = jnp.dot(inputs, w_query, preferred_element_type=jnp.float32).astype(jnp.bfloat16)
    key = jnp.dot(inputs, w_key, preferred_element_type=jnp.float32).astype(jnp.bfloat16)
    value = jnp.dot(inputs, w_value, preferred_element_type=jnp.float32).astype(jnp.bfloat16)
    qh = heads_first(query).astype(jnp.float32)
    kh = heads_first(key).astype(jnp.float32)
    vh = heads_first(value)
    dirs = heads_first(reflect_dir).astype(jnp.float32)
    dirs = dirs * lax.rsqrt(lax.optimization_barrier(jnp.sum(dirs * dirs, axis=-1, keepdims=True)) + 1e-06)
    beta = strength.astype(jnp.float32).reshape(H, SHARDS, TOK)
    counts = jnp.broadcast_to(hop_count[None, :], (H, SHARDS))
    attended = lax.map(single_head, (qh, kh, vh, dirs, beta, counts))
    attended = attended.transpose(1, 2, 0, 3).reshape(TOKENS, H * DH)
    return jnp.dot(attended, w_out, preferred_element_type=jnp.float32).astype(jnp.bfloat16)
```

```python
import jax
import jax.numpy as jnp
from jax import lax
from jax.experimental import pallas as pl
from jax.experimental.pallas import tpu as pltpu
from jax.sharding import PartitionSpec as P

TOK = 256
DH = 128
SCALE = 1.4426950408889634 / DH**0.5
NEG = -1e30
F32 = jnp.float32
BF16 = jnp.bfloat16
HOP_ROW = 3 * TOK + DH
PACK = HOP_ROW + 16
PAIR = 4 * TOK + DH
VMEM = pl.BlockSpec(memory_space=pltpu.VMEM)
SMEM = pl.BlockSpec(memory_space=pltpu.SMEM)

NN = (((1,), (0,)), ((), ()))
NT = (((1,), (1,)), ((), ()))
TN = (((0,), (0,)), ((), ()))


def dot(a, b, dims=NN):
    return lax.dot_general(a, b, dims, preferred_element_type=F32)


def exact(a, b):
    return lax.dot_general(a, b, NN, precision=lax.Precision.HIGHEST, preferred_element_type=F32)


def call(body, outs, ins, scratch=(), flops=0, smem=0):
    return pl.pallas_call(
        body,
        out_shape=outs,
        in_specs=[SMEM] * smem + [VMEM] * (ins - smem),
        out_specs=jax.tree.map(lambda _: VMEM, outs),
        scratch_shapes=list(scratch),
        compiler_params=pltpu.CompilerParams(vmem_limit_bytes=48 * 2**20),
        cost_estimate=pl.CostEstimate(flops=flops, bytes_accessed=2**20, transcendentals=0),
    )


def lower_inverses(blocks, row, col):
    eye = (row == col).astype(F32)
    same = (row // 8) == (col // 8)
    small = [jnp.where(same, b, 0.0) for b in blocks]
    squares = [exact(s, s) for s in small]
    fourths = [exact(s, s) for s in squares]
    firsts = [exact(eye - s, eye + q) for s, q in zip(small, squares)]
    found = [exact(f, eye + q) for f, q in zip(firsts, fourths)]
    size = 8
    while size < DH:
        off = ((row // (2 * size)) == (col // (2 * size))) & ((row // size) != (col // size))
        left = [exact(x, jnp.where(off, b, 0.0)) for x, b in zip(found, blocks)]
        found = [x - exact(y, x) for x, y in zip(found, left)]
        size *= 2
    return found


def directions_kernel(dirs_ref, beta_ref, w_ref, t_ref, u_ref, y_ref, a_ref):
    row = lax.broadcasted_iota(jnp.int32, (TOK, TOK), 0)
    col = lax.broadcasted_iota(jnp.int32, (TOK, TOK), 1)
    strict = row > col
    r, c = row[:DH, :DH], col[:DH, :DH]
    dirs, lows, betas = [], [], []
    for h in range(2):
        d = dirs_ref[:, h * DH : (h + 1) * DH].astype(F32)
        d = d * lax.rsqrt(jnp.sum(d * d, axis=1, keepdims=True) + 1e-6)
        w = d.astype(BF16)
        dirs.append(w)
        beta = beta_ref[h : h + 1, :]
        column = jnp.sum(jnp.where(row == col, beta, 0.0), axis=1, keepdims=True)
        lows.append(jnp.where(strict, dot(w, w, NT) * column, 0.0))
        betas.append(beta)
    corners = []
    for low in lows:
        corners += [low[:DH, :DH], low[DH:, DH:]]
    found = lower_inverses(corners, r, c)
    for h in range(2):
        first, second = found[2 * h], found[2 * h + 1]
        cross = -exact(second, exact(lows[h][DH:, :DH], first))
        upper = jnp.concatenate([first, jnp.zeros((DH, DH), F32)], axis=1)
        lower = jnp.concatenate([cross, second], axis=1)
        t = (jnp.concatenate([upper, lower], axis=0) * betas[h]).astype(BF16)
        w = dirs[h]
        u = dot(t, w, TN).astype(BF16)
        w_ref[h] = w
        t_ref[h] = t
        u_ref[h] = u
        y_ref[h] = dot(t, w).astype(BF16)
        eye = (r == c).astype(F32)
        a_ref[h] = (eye - dot(u, w, TN)).astype(BF16)


def project_kernel(
    at_ref, hop_ref, x_ref, wq_ref, wk_ref, wv_ref, w_ref, u_ref, y_ref, a_ref,
    p0_ref, p1_ref, q_ref, k_ref, v_ref,
):
    def product(weights):
        total = dot(x_ref[0], weights[0:256, :])
        for p in range(1, 8):
            total += dot(x_ref[p], weights[p * 256 : (p + 1) * 256, :])
        return total.astype(BF16)

    query, key, value = product(wq_ref), product(wk_ref), product(wv_ref)
    for h in range(2):
        cut = slice(h * DH, (h + 1) * DH)
        q_ref[h] = query[:, cut]
        k_ref[h] = key[:, cut]
        v_ref[h] = value[:, cut]
    row = lax.broadcasted_iota(jnp.int32, (TOK, TOK), 0)
    col = lax.broadcasted_iota(jnp.int32, (TOK, TOK), 1)
    hops = hop_ref[0].astype(F32)
    for j, p_ref in enumerate((p0_ref, p1_ref)):
        h = lax.rem(at_ref[0] + j, 2)
        q, k, w = q_ref[h], k_ref[h], w_ref[h]
        qdirs = jnp.where(row >= col, dot(q, w, NT), 0.0).astype(BF16)
        keydirs = jnp.where(col > row, dot(k, w, NT), 0.0).astype(BF16)
        qhat = q.astype(F32) - dot(qdirs, y_ref[h])
        p_ref[0:TOK] = (qhat * SCALE).astype(BF16)
        p_ref[TOK : 2 * TOK] = (k.astype(F32) - dot(keydirs, u_ref[h])).astype(BF16)
        p_ref[2 * TOK : 3 * TOK] = v_ref[h]
        p_ref[3 * TOK : HOP_ROW] = a_ref[h]
        p_ref[HOP_ROW:PACK] = jnp.full((16, DH), hops, F32).astype(BF16)


def own_kernel(q_ref, k_ref, v_ref, w_ref, t_ref, acc_ref, lse_ref):
    row = lax.broadcasted_iota(jnp.int32, (TOK, TOK), 0)
    col = lax.broadcasted_iota(jnp.int32, (TOK, TOK), 1)
    for h in range(2):
        q, k, w = q_ref[h], k_ref[h], w_ref[h]
        qdirs = jnp.where(row >= col, dot(q, w, NT), 0.0).astype(BF16)
        dirkeys = jnp.where(row > col, dot(w, k, NT), 0.0).astype(BF16)
        coef = dot(qdirs, t_ref[h]).astype(BF16)
        own = (dot(q, k, NT) - dot(coef, dirkeys)) * SCALE
        own = jnp.where(row >= col, own, NEG)
        top = jnp.max(own, axis=1, keepdims=True)
        prob = jnp.exp2(own - top)
        total = jnp.sum(prob, axis=1, keepdims=True)
        acc_ref[h] = dot(prob.astype(BF16), v_ref[h]) / total
        lse_ref[h] = jnp.broadcast_to(top + jnp.log2(total), (TOK, DH))


def pair_kernel(at_ref, r0_ref, r1_ref, q_ref, pair_ref, hop_ref):
    swapped = at_ref[0] == 1

    def part(low, high):
        a, b = r0_ref[low:high], r1_ref[low:high]
        return jnp.where(swapped, b, a), jnp.where(swapped, a, b)

    q_even, q_odd = part(0, TOK)
    k_even, k_odd = part(TOK, 2 * TOK)
    v_even, v_odd = part(2 * TOK, 3 * TOK)
    a_even, a_odd = part(3 * TOK, HOP_ROW)
    h_even, h_odd = part(HOP_ROW, PACK)
    pair_ref[0:TOK] = dot(k_even, a_odd, NT).astype(BF16)
    pair_ref[TOK : 2 * TOK] = k_odd
    pair_ref[2 * TOK : 3 * TOK] = v_even
    pair_ref[3 * TOK : 4 * TOK] = v_odd
    pair_ref[4 * TOK : PAIR] = dot(a_odd, a_even).astype(BF16)
    q_ref[0, 0] = q_even
    q_ref[0, 1] = q_odd
    q_ref[1, 0] = q_even
    q_ref[1, 1] = dot(q_odd, a_even).astype(BF16)
    q_ref[2, 0] = k_even
    q_ref[2, 1] = v_even
    hop_ref[0] = h_even.astype(F32)
    hop_ref[1] = h_odd.astype(F32)


def mix_kernel(at_ref, a_ref, b_ref, out_ref):
    @pl.when(at_ref[1] == 0)
    def _():
        out_ref[...] = a_ref[...]

    @pl.when(at_ref[1] == 1)
    def _():
        out_ref[...] = b_ref[...]


def window_kernel(
    at_ref, q_ref, hop_ref, z1_ref, z2_ref, s1_ref, s2_ref, o0_ref, o1_ref, scores
):
    keys = (s1_ref, z1_ref, s2_ref, z2_ref)
    pair = at_ref[2]
    col = lax.broadcasted_iota(jnp.int32, (1, 2 * TOK), 1)
    odd_key = col >= TOK
    for j, out_ref in enumerate((o0_ref, o1_ref)):
        i = lax.rem(at_ref[0] + j, 2)
        hops = hop_ref[i, 0:1, 0:1]
        inside = dot(q_ref[0, i], q_ref[2, 0], NT) + jnp.where(i == 1, 0.0, NEG)
        scores[:, 0:TOK] = inside
        top = jnp.max(inside, axis=1, keepdims=True)
        q = q_ref[1, i]
        for d in range(1, 5):
            s = dot(q, keys[d - 1][0 : 2 * TOK], NT)
            distance = 2 * d + i - odd_key.astype(jnp.int32)
            valid = (distance.astype(F32) <= hops) & (pair >= d)
            s = s + jnp.where(valid, 0.0, NEG)
            scores[:, (2 * d - 1) * TOK : (2 * d + 1) * TOK] = s
            top = jnp.maximum(top, jnp.max(s, axis=1, keepdims=True))
            if d < 4:
                q = dot(q, keys[d - 1][4 * TOK : PAIR]).astype(BF16)
        prob = jnp.exp2(scores[:, 0:TOK] - top)
        total = jnp.sum(prob, axis=1, keepdims=True)
        acc = dot(prob.astype(BF16), q_ref[2, 1])
        for d in range(1, 5):
            prob = jnp.exp2(scores[:, (2 * d - 1) * TOK : (2 * d + 1) * TOK] - top)
            total += jnp.sum(prob, axis=1, keepdims=True)
            acc += dot(prob.astype(BF16), keys[d - 1][2 * TOK : 4 * TOK])
        lse = jnp.broadcast_to(top + jnp.log2(total), (TOK, DH))
        high = lse.astype(BF16).astype(F32)
        lane = lax.broadcasted_iota(jnp.int32, (TOK, DH), 1)
        out_ref[:, 0:DH] = (acc / total).astype(BF16)
        out_ref[:, DH:] = jnp.where(lane < DH // 2, high, lse - high).astype(BF16)


def output_kernel(at_ref, g0_ref, g1_ref, acc_ref, lse_ref, wo_ref, out_ref):
    swapped = at_ref[0] == 1
    parts = []
    for h in range(2):
        a, b = (g0_ref, g1_ref) if h == 0 else (g1_ref, g0_ref)
        got = jnp.where(swapped, b[...], a[...]).astype(F32)
        far = got[:, DH : DH + 1] + got[:, DH + DH // 2 : DH + DH // 2 + 1]
        own = lse_ref[h, :, 0:1]
        top = jnp.maximum(own, far)
        mine, theirs = jnp.exp2(own - top), jnp.exp2(far - top)
        mixed = (acc_ref[h] * mine + got[:, :DH] * theirs) / (mine + theirs)
        parts.append(mixed.astype(BF16))
    attended = jnp.concatenate(parts, axis=1)
    for p in range(8):
        out_ref[p] = dot(attended, wo_ref[:, p * 256 : (p + 1) * 256]).astype(BF16)


def sum_kernel(x_ref, out_ref):
    total = x_ref[0].astype(F32)
    for p in range(1, 8):
        total += x_ref[p].astype(F32)
    out_ref[...] = total.astype(BF16)


def regroup_pairs(j, rows, cross, groups):
    pairs = []
    for z in range(rows):
        for x in range(4):
            for y in range(groups):
                for c in range(2):
                    i = (x + j) % 2
                    pairs.append(((z * 4 + x) * cross + y * 2 + c, (z * 4 + 2 * c + i) * cross + y * 2 + x // 2))
    return pairs


def shape(dims, dtype=BF16):
    return jax.ShapeDtypeStruct(dims, dtype)


def shards(inputs, w_query, w_key, w_value, w_out, reflect_dir, strength, hop_count):
    both = ("ctx", "head")
    z = lax.axis_index("ctx") // 4
    x = lax.axis_index("ctx") % 4
    c = lax.axis_index("head") % 2
    at = jnp.stack([x % 2, c, 2 * z + c]).astype(jnp.int32)
    there = [regroup_pairs(j, 16, 8, 4) for j in range(2)]
    back = [[(b, a) for a, b in pairs] for pairs in there]
    down = [(b, b + 4) for b in range(60)]
    twin = [(h, h ^ 1) for h in range(8)]

    w, t, u, y, a = call(
        directions_kernel,
        [shape((2, TOK, DH)), shape((2, TOK, TOK)), shape((2, TOK, DH)), shape((2, TOK, DH)), shape((2, DH, DH))],
        2, flops=2**32,
    )(reflect_dir, strength)
    gathered = lax.all_to_all(jnp.broadcast_to(inputs[None], (8, TOK, 256)), "head", 0, 0)
    p0, p1, q, k, v = call(
        project_kernel,
        [shape((PACK, DH)), shape((PACK, DH))] + [shape((2, TOK, DH))] * 3,
        10, smem=2, flops=2**30,
    )(at, hop_count, gathered, w_query, w_key, w_value, w, u, y, a)
    r0 = lax.ppermute(p0, both, there[0])
    r1 = lax.ppermute(p1, both, there[1])
    acc, lse = call(
        own_kernel, [shape((2, TOK, DH), F32), shape((2, TOK, DH), F32)], 5, flops=2**31
    )(q, k, v, w, t)
    qs, own_pair, hops = call(
        pair_kernel,
        [shape((3, 2, TOK, DH)), shape((PAIR, DH)), shape((2, 16, DH), F32)],
        3, smem=1, flops=2**28,
    )(at, r0, r1)
    mix = call(mix_kernel, shape((PAIR, DH)), 3, smem=1, flops=2**27)
    z1 = lax.ppermute(own_pair, "ctx", down)
    z2 = lax.ppermute(z1, "ctx", down)
    s1 = lax.ppermute(mix(at, own_pair, z1), "head", twin)
    s2 = lax.ppermute(mix(at, z1, z2), "head", twin)
    o0, o1 = call(
        window_kernel,
        [shape((TOK, 2 * DH)), shape((TOK, 2 * DH))],
        7, smem=1, flops=2**30,
        scratch=[pltpu.VMEM((TOK, 9 * TOK), F32)],
    )(at, qs, hops, z1, z2, s1, s2)
    g0 = lax.ppermute(o0, both, back[0])
    g1 = lax.ppermute(o1, both, back[1])
    partial = call(output_kernel, shape((8, TOK, 256)), 6, smem=1, flops=2**29)(at, g0, g1, acc, lse, w_out)
    pieces = lax.all_to_all(partial, "head", 0, 0)
    return call(sum_kernel, shape((TOK, 256)), 1)(pieces)


def solution(mesh):
    placed = (
        P("ctx", "head"),
        P(None, "head"),
        P(None, "head"),
        P(None, "head"),
        P("head", None),
        P("ctx", "head"),
        P("head", "ctx"),
        P("ctx"),
    )
    return jax.shard_map(
        shards, mesh=mesh, in_specs=placed, out_specs=P("ctx", "head"), check_vma=False
    )
```

```python
import jax
import jax.numpy as jnp
from jax import lax
from jax.experimental import pallas as pl
from jax.experimental.pallas import tpu as pltpu
from jax.sharding import PartitionSpec as P

TOK = 256
DH = 128
SCALE = 1.4426950408889634 / DH**0.5
NEG = -1e30
F32 = jnp.float32
BF16 = jnp.bfloat16
HOP_ROW = 3 * TOK + DH
PACK = HOP_ROW + 16
PAIR = 4 * TOK + DH
BACK = TOK + 16
VMEM = pl.BlockSpec(memory_space=pltpu.VMEM)
SMEM = pl.BlockSpec(memory_space=pltpu.SMEM)

NN = (((1,), (0,)), ((), ()))
NT = (((1,), (1,)), ((), ()))
TN = (((0,), (0,)), ((), ()))


def dot(a, b, dims=NN):
    return lax.dot_general(a, b, dims, preferred_element_type=F32)


def exact(a, b):
    return lax.dot_general(a, b, NN, precision=lax.Precision.HIGHEST, preferred_element_type=F32)


def call(body, outs, ins, flops=0, smem=0):
    return pl.pallas_call(
        body,
        out_shape=outs,
        in_specs=[SMEM] * smem + [VMEM] * (ins - smem),
        out_specs=jax.tree.map(lambda _: VMEM, outs),
        compiler_params=pltpu.CompilerParams(vmem_limit_bytes=48 * 2**20),
        cost_estimate=pl.CostEstimate(flops=flops, bytes_accessed=2**20, transcendentals=0),
    )


def lower_inverses(blocks, row, col):
    eye = (row == col).astype(F32)
    same = (row // 8) == (col // 8)
    small = [jnp.where(same, b, 0.0) for b in blocks]
    squares = [exact(s, s) for s in small]
    fourths = [exact(s, s) for s in squares]
    firsts = [exact(eye - s, eye + q) for s, q in zip(small, squares)]
    found = [exact(f, eye + q) for f, q in zip(firsts, fourths)]
    size = 8
    while size < DH:
        off = ((row // (2 * size)) == (col // (2 * size))) & ((row // size) != (col // size))
        left = [exact(x, jnp.where(off, b, 0.0)) for x, b in zip(found, blocks)]
        found = [x - exact(y, x) for x, y in zip(found, left)]
        size *= 2
    return found


def directions_kernel(dirs_ref, beta_ref, w_ref, t_ref, u_ref, y_ref, a_ref):
    row = lax.broadcasted_iota(jnp.int32, (TOK, TOK), 0)
    col = lax.broadcasted_iota(jnp.int32, (TOK, TOK), 1)
    strict = row > col
    r, c = row[:DH, :DH], col[:DH, :DH]
    dirs, lows, betas = [], [], []
    for h in range(2):
        d = dirs_ref[:, h * DH : (h + 1) * DH].astype(F32)
        d = d * lax.rsqrt(jnp.sum(d * d, axis=1, keepdims=True) + 1e-6)
        w = d.astype(BF16)
        dirs.append(w)
        beta = beta_ref[h : h + 1, :]
        column = jnp.sum(jnp.where(row == col, beta, 0.0), axis=1, keepdims=True)
        lows.append(jnp.where(strict, dot(w, w, NT) * column, 0.0))
        betas.append(beta)
    corners = []
    for low in lows:
        corners += [low[:DH, :DH], low[DH:, DH:]]
    found = lower_inverses(corners, r, c)
    for h in range(2):
        first, second = found[2 * h], found[2 * h + 1]
        cross = -exact(second, exact(lows[h][DH:, :DH], first))
        upper = jnp.concatenate([first, jnp.zeros((DH, DH), F32)], axis=1)
        lower = jnp.concatenate([cross, second], axis=1)
        t = (jnp.concatenate([upper, lower], axis=0) * betas[h]).astype(BF16)
        w = dirs[h]
        u = dot(t, w, TN).astype(BF16)
        w_ref[h] = w
        t_ref[h] = t
        u_ref[h] = u
        y_ref[h] = dot(t, w).astype(BF16)
        eye = (r == c).astype(F32)
        a_ref[h] = (eye - dot(u, w, TN)).astype(BF16)


def project_kernel(
    at_ref, hop_ref, x_ref, o_ref, wq_ref, wk_ref, wv_ref, w_ref, u_ref, y_ref, a_ref,
    p0_ref, p1_ref, q_ref, k_ref, v_ref,
):
    def product(weights):
        total = None
        for p in range(4):
            for ref, c in ((x_ref, at_ref[1]), (o_ref, 1 - at_ref[1])):
                rows = pl.ds(pl.multiple_of((2 * p + c) * 256, 256), 256)
                term = dot(ref[p], weights[rows, :])
                total = term if total is None else total + term
        return total.astype(BF16)

    query, key, value = product(wq_ref), product(wk_ref), product(wv_ref)
    for h in range(2):
        cut = slice(h * DH, (h + 1) * DH)
        q_ref[h] = query[:, cut]
        k_ref[h] = key[:, cut]
        v_ref[h] = value[:, cut]
    row = lax.broadcasted_iota(jnp.int32, (TOK, TOK), 0)
    col = lax.broadcasted_iota(jnp.int32, (TOK, TOK), 1)
    hops = hop_ref[0].astype(F32)
    for j, p_ref in enumerate((p0_ref, p1_ref)):
        h = lax.rem(at_ref[0] + j, 2)
        q, k, w = q_ref[h], k_ref[h], w_ref[h]
        qdirs = jnp.where(row >= col, dot(q, w, NT), 0.0).astype(BF16)
        keydirs = jnp.where(col > row, dot(k, w, NT), 0.0).astype(BF16)
        qhat = q.astype(F32) - dot(qdirs, y_ref[h])
        p_ref[0:TOK] = (qhat * SCALE).astype(BF16)
        p_ref[TOK : 2 * TOK] = (k.astype(F32) - dot(keydirs, u_ref[h])).astype(BF16)
        p_ref[2 * TOK : 3 * TOK] = v_ref[h]
        p_ref[3 * TOK : HOP_ROW] = a_ref[h]
        p_ref[HOP_ROW:PACK] = jnp.full((16, DH), hops, F32).astype(BF16)


def own_kernel(q_ref, k_ref, v_ref, w_ref, t_ref, acc_ref, lse_ref):
    row = lax.broadcasted_iota(jnp.int32, (TOK, TOK), 0)
    col = lax.broadcasted_iota(jnp.int32, (TOK, TOK), 1)
    for h in range(2):
        q, k, w = q_ref[h], k_ref[h], w_ref[h]
        qdirs = jnp.where(row >= col, dot(q, w, NT), 0.0).astype(BF16)
        dirkeys = jnp.where(row > col, dot(w, k, NT), 0.0).astype(BF16)
        coef = dot(qdirs, t_ref[h]).astype(BF16)
        own = (dot(q, k, NT) - dot(coef, dirkeys)) * SCALE
        own = jnp.where(row >= col, own, NEG)
        top = jnp.max(own, axis=1, keepdims=True)
        prob = jnp.exp2(own - top)
        total = jnp.sum(prob, axis=1, keepdims=True)
        acc_ref[h] = dot(prob.astype(BF16), v_ref[h]) / total
        lse_ref[h] = jnp.broadcast_to(top + jnp.log2(total), (TOK, DH))


def pair_kernel(at_ref, r0_ref, r1_ref, q_ref, pair_ref, hop_ref):
    swapped = at_ref[0] == 1

    def part(low, high):
        a, b = r0_ref[low:high], r1_ref[low:high]
        return jnp.where(swapped, b, a), jnp.where(swapped, a, b)

    q_even, q_odd = part(0, TOK)
    k_even, k_odd = part(TOK, 2 * TOK)
    v_even, v_odd = part(2 * TOK, 3 * TOK)
    a_even, a_odd = part(3 * TOK, HOP_ROW)
    h_even, h_odd = part(HOP_ROW, PACK)
    pair_ref[0:TOK] = dot(k_even, a_odd, NT).astype(BF16)
    pair_ref[TOK : 2 * TOK] = k_odd
    pair_ref[2 * TOK : 3 * TOK] = v_even
    pair_ref[3 * TOK : 4 * TOK] = v_odd
    pair_ref[4 * TOK : PAIR] = dot(a_odd, a_even).astype(BF16)
    q_ref[0, 0] = q_even
    q_ref[0, 1] = q_odd
    q_ref[1, 0] = q_even
    q_ref[1, 1] = dot(q_odd, a_even).astype(BF16)
    q_ref[2, 0] = k_even
    q_ref[2, 1] = v_even
    hop_ref[0] = h_even.astype(F32)
    hop_ref[1] = h_odd.astype(F32)


def window_step(q, keys, d, i, hops, pair):
    col = lax.broadcasted_iota(jnp.int32, (1, 2 * TOK), 1)
    distance = 2 * d + i - (col >= TOK).astype(jnp.int32)
    valid = (distance.astype(F32) <= hops) & (pair >= d)
    return dot(q, keys[0 : 2 * TOK], NT) + jnp.where(valid, 0.0, NEG)


def near_kernel(at_ref, q_ref, hop_ref, d1_ref, d2_ref, acc_ref, top_ref, total_ref, next_ref):
    pair = at_ref[2]
    for i in range(2):
        hops = hop_ref[i, 0:1, 0:1]
        q = q_ref[1, i]
        first = window_step(q, d1_ref, 1, i, hops, pair)
        q = dot(q, d1_ref[4 * TOK : PAIR]).astype(BF16)
        second = window_step(q, d2_ref, 2, i, hops, pair)
        next_ref[i] = dot(q, d2_ref[4 * TOK : PAIR]).astype(BF16)
        top = jnp.maximum(jnp.max(first, axis=1, keepdims=True), jnp.max(second, axis=1, keepdims=True))
        if i == 1:
            inside = dot(q_ref[0, 1], q_ref[2, 0], NT)
            top = jnp.maximum(top, jnp.max(inside, axis=1, keepdims=True))
        first, second = jnp.exp2(first - top), jnp.exp2(second - top)
        total = jnp.sum(first, axis=1, keepdims=True) + jnp.sum(second, axis=1, keepdims=True)
        acc = dot(first.astype(BF16), d1_ref[2 * TOK : 4 * TOK])
        acc += dot(second.astype(BF16), d2_ref[2 * TOK : 4 * TOK])
        if i == 1:
            inside = jnp.exp2(inside - top)
            total += jnp.sum(inside, axis=1, keepdims=True)
            acc += dot(inside.astype(BF16), q_ref[2, 1])
        acc_ref[i] = acc
        top_ref[i] = jnp.broadcast_to(top, (TOK, DH))
        total_ref[i] = jnp.broadcast_to(total, (TOK, DH))


def far_kernel(
    at_ref, hop_ref, d3_ref, d4_ref, acc_ref, top_ref, total_ref, next_ref, o0_ref, o1_ref
):
    pair = at_ref[2]
    for j, out_ref in enumerate((o0_ref, o1_ref)):
        i = lax.rem(at_ref[0] + j, 2)
        hops = hop_ref[i, 0:1, 0:1]
        q = next_ref[i]
        third = window_step(q, d3_ref, 3, i, hops, pair)
        q = dot(q, d3_ref[4 * TOK : PAIR]).astype(BF16)
        fourth = window_step(q, d4_ref, 4, i, hops, pair)
        before = top_ref[i, :, 0:1]
        top = jnp.maximum(jnp.max(third, axis=1, keepdims=True), jnp.max(fourth, axis=1, keepdims=True))
        top = jnp.maximum(top, before)
        third, fourth = jnp.exp2(third - top), jnp.exp2(fourth - top)
        kept = jnp.exp2(before - top)
        total = total_ref[i, :, 0:1] * kept
        total += jnp.sum(third, axis=1, keepdims=True) + jnp.sum(fourth, axis=1, keepdims=True)
        acc = acc_ref[i] * kept
        acc += dot(third.astype(BF16), d3_ref[2 * TOK : 4 * TOK])
        acc += dot(fourth.astype(BF16), d4_ref[2 * TOK : 4 * TOK])
        out_ref[0:TOK] = (acc / total).astype(BF16)
        lse = jnp.broadcast_to(top + jnp.log2(total), (TOK, DH)).T[0:16]
        high = lse.astype(BF16).astype(F32)
        low = lse - high
        line = lax.broadcasted_iota(jnp.int32, (16, DH), 0)
        tile = jnp.where(line == 0, high[:, :DH], high[:, DH:])
        tile = jnp.where(line == 2, low[:, :DH], tile)
        tile = jnp.where(line == 3, low[:, DH:], tile)
        out_ref[TOK:BACK] = tile.astype(BF16)


def merge_kernel(at_ref, g0_ref, g1_ref, acc_ref, lse_ref, out_ref):
    swapped = at_ref[0] == 1
    row = lax.broadcasted_iota(jnp.int32, (DH, DH), 0)
    col = lax.broadcasted_iota(jnp.int32, (DH, DH), 1)
    for h in range(2):
        a, b = (g0_ref, g1_ref) if h == 0 else (g1_ref, g0_ref)
        got = jnp.where(swapped, b[...], a[...]).astype(F32)
        tile = got[TOK:BACK]
        column = []
        for part in range(2):
            line = tile[part : part + 1] + tile[part + 2 : part + 3]
            column.append(jnp.sum(jnp.where(row == col, line, 0.0), axis=1, keepdims=True))
        far = jnp.concatenate(column, axis=0)
        own = lse_ref[h, :, 0:1]
        top = jnp.maximum(own, far)
        mine, theirs = jnp.exp2(own - top), jnp.exp2(far - top)
        mixed = (acc_ref[h] * mine + got[:TOK] * theirs) / (mine + theirs)
        out_ref[:, h * DH : (h + 1) * DH] = mixed.astype(BF16)


def columns(c, p):
    return pl.ds(pl.multiple_of((2 * p + c) * 256, 256), 256)


def halves_kernel(at_ref, wo_ref, out_ref):
    for p in range(4):
        out_ref[p] = wo_ref[:, columns(1 - at_ref[1], p)]


def output_kernel(at_ref, mine_ref, theirs_ref, wo_ref, other_ref, out_ref):
    for p in range(4):
        total = dot(mine_ref[...], wo_ref[:, columns(at_ref[1], p)])
        out_ref[p] = (total + dot(theirs_ref[...], other_ref[p])).astype(BF16)


def sum_kernel(x_ref, out_ref):
    total = x_ref[0].astype(F32)
    for p in range(1, 4):
        total += x_ref[p].astype(F32)
    out_ref[...] = total.astype(BF16)


def regroup_pairs(j, rows, cross, groups):
    pairs = []
    for z in range(rows):
        for x in range(4):
            for y in range(groups):
                for c in range(2):
                    i = (x + j) % 2
                    pairs.append(((z * 4 + x) * cross + y * 2 + c, (z * 4 + 2 * c + i) * cross + y * 2 + x // 2))
    return pairs


def follow_pairs(rows, cross):
    pairs = []
    for b in range(4 * rows):
        for y in range(0, cross, 2):
            pairs.append((b * cross + y, b * cross + y + 1))
            if b + 4 < 4 * rows:
                pairs.append((b * cross + y + 1, (b + 4) * cross + y))
    return pairs


def shape(dims, dtype=BF16):
    return jax.ShapeDtypeStruct(dims, dtype)


def shards(inputs, w_query, w_key, w_value, w_out, reflect_dir, strength, hop_count):
    both = ("ctx", "head")
    z = lax.axis_index("ctx") // 4
    x = lax.axis_index("ctx") % 4
    c = lax.axis_index("head") % 2
    at = jnp.stack([x % 2, c, 2 * z + c]).astype(jnp.int32)
    there = [regroup_pairs(j, 16, 8, 4) for j in range(2)]
    back = [[(b, a) for a, b in pairs] for pairs in there]
    follow = follow_pairs(16, 8)
    down = [(b, b + 4) for b in range(60)]
    twin = [(h, h ^ 1) for h in range(8)]

    w, t, u, y, a = call(
        directions_kernel,
        [shape((2, TOK, DH)), shape((2, TOK, TOK)), shape((2, TOK, DH)), shape((2, TOK, DH)), shape((2, DH, DH))],
        2, flops=2**32,
    )(reflect_dir, strength)
    planes = [[0, 2, 4, 6], [1, 3, 5, 7]]
    copies = jnp.broadcast_to(inputs[None], (4, TOK, 256))
    gathered = lax.all_to_all(copies, "head", 0, 0, axis_index_groups=planes)
    other = lax.ppermute(gathered, "head", twin)
    halves = call(halves_kernel, shape((4, 256, 256)), 2, smem=1)(at, w_out)
    other_out = lax.ppermute(halves, "head", twin)
    p0, p1, q, k, v = call(
        project_kernel,
        [shape((PACK, DH)), shape((PACK, DH))] + [shape((2, TOK, DH))] * 3,
        11, smem=2, flops=2**30,
    )(at, hop_count, gathered, other, w_query, w_key, w_value, w, u, y, a)
    r0 = lax.ppermute(p0, both, there[0])
    r1 = lax.ppermute(p1, both, there[1])
    acc, lse = call(
        own_kernel, [shape((2, TOK, DH), F32), shape((2, TOK, DH), F32)], 5, flops=2**31
    )(q, k, v, w, t)
    qs, own_pair, hops = call(
        pair_kernel,
        [shape((3, 2, TOK, DH)), shape((PAIR, DH)), shape((2, 16, DH), F32)],
        3, smem=1, flops=2**28,
    )(at, r0, r1)
    d1 = lax.ppermute(own_pair, both, follow)
    d2 = lax.ppermute(own_pair, "ctx", down)
    d3 = lax.ppermute(d2, both, follow)
    d4 = lax.ppermute(d2, "ctx", down)
    state = [shape((2, TOK, DH), F32)] * 3 + [shape((2, TOK, DH))]
    near = call(near_kernel, state, 5, smem=1, flops=2**31)(at, qs, hops, d1, d2)
    o0, o1 = call(
        far_kernel, [shape((BACK, DH)), shape((BACK, DH))], 8, smem=1, flops=2**30
    )(at, hops, d3, d4, *near)
    g0 = lax.ppermute(o0, both, back[0])
    g1 = lax.ppermute(o1, both, back[1])
    mine = call(merge_kernel, shape((TOK, 2 * DH)), 5, smem=1, flops=2**28)(at, g0, g1, acc, lse)
    theirs = lax.ppermute(mine, "head", twin)
    partial = call(output_kernel, shape((4, TOK, 256)), 5, smem=1, flops=2**29)(
        at, mine, theirs, w_out, other_out
    )
    pieces = lax.all_to_all(partial, "head", 0, 0, axis_index_groups=planes)
    return call(sum_kernel, shape((TOK, 256)), 1)(pieces)


def solution(mesh):
    placed = (
        P("ctx", "head"),
        P(None, "head"),
        P(None, "head"),
        P(None, "head"),
        P("head", None),
        P("ctx", "head"),
        P("head", "ctx"),
        P("ctx"),
    )
    return jax.shard_map(
        shards, mesh=mesh, in_specs=placed, out_specs=P("ctx", "head"), check_vma=False
    )
```

```python
import jax
import jax.numpy as jnp
from jax import lax
from jax.experimental import pallas as pl
from jax.experimental.pallas import tpu as pltpu
from jax.sharding import PartitionSpec as P

TOK = 256
DH = 128
SCALE = 1.4426950408889634 / DH**0.5
NEG = -1e30
F32 = jnp.float32
BF16 = jnp.bfloat16
HOP_ROW = 3 * TOK + DH
PACK = HOP_ROW + 16
PAIR = 4 * TOK + DH
BACK = TOK + 16
VMEM = pl.BlockSpec(memory_space=pltpu.VMEM)
SMEM = pl.BlockSpec(memory_space=pltpu.SMEM)

NN = (((1,), (0,)), ((), ()))
NT = (((1,), (1,)), ((), ()))
TN = (((0,), (0,)), ((), ()))


def dot(a, b, dims=NN):
    return lax.dot_general(a, b, dims, preferred_element_type=F32)


def split(a):
    high = a.astype(BF16)
    return high, (a - high.astype(F32)).astype(BF16)


def exact(a, b):
    (ah, al), (bh, bl) = split(a), split(b)
    return dot(ah, bh) + (dot(ah, bl) + dot(al, bh))


def call(body, outs, ins, flops=0, smem=0):
    return pl.pallas_call(
        body,
        out_shape=outs,
        in_specs=[SMEM] * smem + [VMEM] * (ins - smem),
        out_specs=jax.tree.map(lambda _: VMEM, outs),
        compiler_params=pltpu.CompilerParams(vmem_limit_bytes=48 * 2**20),
        cost_estimate=pl.CostEstimate(flops=flops, bytes_accessed=2**20, transcendentals=0),
    )


def lower_inverses(blocks, row, col):
    eye = (row == col).astype(F32)
    same = (row // 4) == (col // 4)
    small = [jnp.where(same, b, 0.0) for b in blocks]
    squares = [exact(s, s) for s in small]
    found = [exact(eye - s, eye + q) for s, q in zip(small, squares)]
    size = 4
    while size < DH:
        off = ((row // (2 * size)) == (col // (2 * size))) & ((row // size) != (col // size))
        left = [exact(x, jnp.where(off, b, 0.0)) for x, b in zip(found, blocks)]
        found = [x - exact(y, x) for x, y in zip(found, left)]
        size *= 2
    return found


def directions_kernel(dirs_ref, beta_ref, w_ref, t_ref, u_ref, y_ref, a_ref):
    row = lax.broadcasted_iota(jnp.int32, (TOK, TOK), 0)
    col = lax.broadcasted_iota(jnp.int32, (TOK, TOK), 1)
    strict = row > col
    r, c = row[:DH, :DH], col[:DH, :DH]
    dirs, lows, betas = [], [], []
    for h in range(2):
        d = dirs_ref[:, h * DH : (h + 1) * DH].astype(F32)
        d = d * lax.rsqrt(jnp.sum(d * d, axis=1, keepdims=True) + 1e-6)
        w = d.astype(BF16)
        dirs.append(w)
        beta = beta_ref[h : h + 1, :]
        column = jnp.sum(jnp.where(row == col, beta, 0.0), axis=1, keepdims=True)
        lows.append(jnp.where(strict, dot(w, w, NT) * column, 0.0))
        betas.append(beta)
    corners = []
    for low in lows:
        corners += [low[:DH, :DH], low[DH:, DH:]]
    found = lower_inverses(corners, r, c)
    for h in range(2):
        first, second = found[2 * h], found[2 * h + 1]
        cross = -exact(second, exact(lows[h][DH:, :DH], first))
        upper = jnp.concatenate([first, jnp.zeros((DH, DH), F32)], axis=1)
        lower = jnp.concatenate([cross, second], axis=1)
        t = (jnp.concatenate([upper, lower], axis=0) * betas[h]).astype(BF16)
        w = dirs[h]
        u = dot(t, w, TN).astype(BF16)
        w_ref[h] = w
        t_ref[h] = t
        u_ref[h] = u
        y_ref[h] = dot(t, w).astype(BF16)
        eye = (r == c).astype(F32)
        a_ref[h] = (eye - dot(u, w, TN)).astype(BF16)


def project_kernel(
    at_ref, hop_ref, x_ref, o_ref, wq_ref, wk_ref, wv_ref, w_ref, u_ref, y_ref, a_ref,
    p0_ref, p1_ref, q_ref, k_ref, v_ref,
):
    def product(weights):
        total = None
        for p in range(4):
            for ref, c in ((x_ref, at_ref[1]), (o_ref, 1 - at_ref[1])):
                rows = pl.ds(pl.multiple_of((2 * p + c) * 256, 256), 256)
                term = dot(ref[p], weights[rows, :])
                total = term if total is None else total + term
        return total.astype(BF16)

    query, key, value = product(wq_ref), product(wk_ref), product(wv_ref)
    for h in range(2):
        cut = slice(h * DH, (h + 1) * DH)
        q_ref[h] = query[:, cut]
        k_ref[h] = key[:, cut]
        v_ref[h] = value[:, cut]
    row = lax.broadcasted_iota(jnp.int32, (TOK, TOK), 0)
    col = lax.broadcasted_iota(jnp.int32, (TOK, TOK), 1)
    hops = hop_ref[0].astype(F32)
    for j, p_ref in enumerate((p0_ref, p1_ref)):
        h = lax.rem(at_ref[0] + j, 2)
        q, k, w = q_ref[h], k_ref[h], w_ref[h]
        qdirs = jnp.where(row >= col, dot(q, w, NT), 0.0).astype(BF16)
        keydirs = jnp.where(col > row, dot(k, w, NT), 0.0).astype(BF16)
        qhat = q.astype(F32) - dot(qdirs, y_ref[h])
        p_ref[0:TOK] = (qhat * SCALE).astype(BF16)
        p_ref[TOK : 2 * TOK] = (k.astype(F32) - dot(keydirs, u_ref[h])).astype(BF16)
        p_ref[2 * TOK : 3 * TOK] = v_ref[h]
        p_ref[3 * TOK : HOP_ROW] = a_ref[h]
        p_ref[HOP_ROW:PACK] = jnp.full((16, DH), hops, F32).astype(BF16)


def own_kernel(q_ref, k_ref, v_ref, w_ref, t_ref, acc_ref, lse_ref):
    row = lax.broadcasted_iota(jnp.int32, (TOK, TOK), 0)
    col = lax.broadcasted_iota(jnp.int32, (TOK, TOK), 1)
    for h in range(2):
        q, k, w = q_ref[h], k_ref[h], w_ref[h]
        qdirs = jnp.where(row >= col, dot(q, w, NT), 0.0).astype(BF16)
        dirkeys = jnp.where(row > col, dot(w, k, NT), 0.0).astype(BF16)
        coef = dot(qdirs, t_ref[h]).astype(BF16)
        own = (dot(q, k, NT) - dot(coef, dirkeys)) * SCALE
        own = jnp.where(row >= col, own, NEG)
        top = jnp.max(own, axis=1, keepdims=True)
        prob = jnp.exp2(own - top)
        total = jnp.sum(prob, axis=1, keepdims=True)
        acc_ref[h] = dot(prob.astype(BF16), v_ref[h]) / total
        lse_ref[h] = jnp.broadcast_to(top + jnp.log2(total), (TOK, DH))


def pair_kernel(at_ref, r0_ref, r1_ref, q_ref, pair_ref, hop_ref):
    swapped = at_ref[0] == 1

    def part(low, high):
        a, b = r0_ref[low:high], r1_ref[low:high]
        return jnp.where(swapped, b, a), jnp.where(swapped, a, b)

    q_even, q_odd = part(0, TOK)
    k_even, k_odd = part(TOK, 2 * TOK)
    v_even, v_odd = part(2 * TOK, 3 * TOK)
    a_even, a_odd = part(3 * TOK, HOP_ROW)
    h_even, h_odd = part(HOP_ROW, PACK)
    pair_ref[0:TOK] = dot(k_even, a_odd, NT).astype(BF16)
    pair_ref[TOK : 2 * TOK] = k_odd
    pair_ref[2 * TOK : 3 * TOK] = v_even
    pair_ref[3 * TOK : 4 * TOK] = v_odd
    pair_ref[4 * TOK : PAIR] = dot(a_odd, a_even).astype(BF16)
    q_ref[0, 0] = q_even
    q_ref[0, 1] = q_odd
    q_ref[1, 0] = q_even
    q_ref[1, 1] = dot(q_odd, a_even).astype(BF16)
    q_ref[2, 0] = k_even
    q_ref[2, 1] = v_even
    hop_ref[0] = h_even.astype(F32)
    hop_ref[1] = h_odd.astype(F32)


def window_step(q, keys, d, i, hops, pair):
    col = lax.broadcasted_iota(jnp.int32, (1, 2 * TOK), 1)
    distance = 2 * d + i - (col >= TOK).astype(jnp.int32)
    valid = (distance.astype(F32) <= hops) & (pair >= d)
    return dot(q, keys[0 : 2 * TOK], NT) + jnp.where(valid, 0.0, NEG)


def near_kernel(at_ref, q_ref, hop_ref, d1_ref, d2_ref, acc_ref, top_ref, total_ref, next_ref):
    pair = at_ref[2]
    for i in range(2):
        hops = hop_ref[i, 0:1, 0:1]
        q = q_ref[1, i]
        first = window_step(q, d1_ref, 1, i, hops, pair)
        q = dot(q, d1_ref[4 * TOK : PAIR]).astype(BF16)
        second = window_step(q, d2_ref, 2, i, hops, pair)
        next_ref[i] = dot(q, d2_ref[4 * TOK : PAIR]).astype(BF16)
        top = jnp.maximum(jnp.max(first, axis=1, keepdims=True), jnp.max(second, axis=1, keepdims=True))
        if i == 1:
            inside = dot(q_ref[0, 1], q_ref[2, 0], NT)
            top = jnp.maximum(top, jnp.max(inside, axis=1, keepdims=True))
        first, second = jnp.exp2(first - top), jnp.exp2(second - top)
        total = jnp.sum(first, axis=1, keepdims=True) + jnp.sum(second, axis=1, keepdims=True)
        acc = dot(first.astype(BF16), d1_ref[2 * TOK : 4 * TOK])
        acc += dot(second.astype(BF16), d2_ref[2 * TOK : 4 * TOK])
        if i == 1:
            inside = jnp.exp2(inside - top)
            total += jnp.sum(inside, axis=1, keepdims=True)
            acc += dot(inside.astype(BF16), q_ref[2, 1])
        acc_ref[i] = acc
        top_ref[i] = jnp.broadcast_to(top, (TOK, DH))
        total_ref[i] = jnp.broadcast_to(total, (TOK, DH))


def far_kernel(
    at_ref, hop_ref, d3_ref, d4_ref, acc_ref, top_ref, total_ref, next_ref, out_ref
):
    pair = at_ref[2]
    for i in range(2):
        piece = 2 * at_ref[1] + i
        hops = hop_ref[i, 0:1, 0:1]
        q = next_ref[i]
        third = window_step(q, d3_ref, 3, i, hops, pair)
        q = dot(q, d3_ref[4 * TOK : PAIR]).astype(BF16)
        fourth = window_step(q, d4_ref, 4, i, hops, pair)
        before = top_ref[i, :, 0:1]
        top = jnp.maximum(jnp.max(third, axis=1, keepdims=True), jnp.max(fourth, axis=1, keepdims=True))
        top = jnp.maximum(top, before)
        third, fourth = jnp.exp2(third - top), jnp.exp2(fourth - top)
        kept = jnp.exp2(before - top)
        total = total_ref[i, :, 0:1] * kept
        total += jnp.sum(third, axis=1, keepdims=True) + jnp.sum(fourth, axis=1, keepdims=True)
        acc = acc_ref[i] * kept
        acc += dot(third.astype(BF16), d3_ref[2 * TOK : 4 * TOK])
        acc += dot(fourth.astype(BF16), d4_ref[2 * TOK : 4 * TOK])
        out_ref[piece, 0:TOK] = (acc / total).astype(BF16)
        lse = jnp.broadcast_to(top + jnp.log2(total), (TOK, DH)).T[0:16]
        high = lse.astype(BF16).astype(F32)
        low = lse - high
        line = lax.broadcasted_iota(jnp.int32, (16, DH), 0)
        tile = jnp.where(line == 0, high[:, :DH], high[:, DH:])
        tile = jnp.where(line == 2, low[:, :DH], tile)
        tile = jnp.where(line == 3, low[:, DH:], tile)
        out_ref[piece, TOK:BACK] = tile.astype(BF16)
        out_ref[2 * (1 - at_ref[1]) + i] = jnp.zeros((BACK, DH), BF16)


def merge_kernel(at_ref, g_ref, acc_ref, lse_ref, out_ref):
    row = lax.broadcasted_iota(jnp.int32, (DH, DH), 0)
    col = lax.broadcasted_iota(jnp.int32, (DH, DH), 1)
    for h in range(2):
        got = g_ref[2 * at_ref[1] + h].astype(F32)
        tile = got[TOK:BACK]
        column = []
        for part in range(2):
            line = tile[part : part + 1] + tile[part + 2 : part + 3]
            column.append(jnp.sum(jnp.where(row == col, line, 0.0), axis=1, keepdims=True))
        far = jnp.concatenate(column, axis=0)
        own = lse_ref[h, :, 0:1]
        top = jnp.maximum(own, far)
        mine, theirs = jnp.exp2(own - top), jnp.exp2(far - top)
        mixed = (acc_ref[h] * mine + got[:TOK] * theirs) / (mine + theirs)
        out_ref[:, h * DH : (h + 1) * DH] = mixed.astype(BF16)


def columns(c, p):
    return pl.ds(pl.multiple_of((2 * p + c) * 256, 256), 256)


def halves_kernel(at_ref, wo_ref, out_ref):
    for p in range(4):
        out_ref[p] = wo_ref[:, columns(1 - at_ref[1], p)]


def output_kernel(at_ref, mine_ref, theirs_ref, wo_ref, other_ref, out_ref):
    for p in range(4):
        total = dot(mine_ref[...], wo_ref[:, columns(at_ref[1], p)])
        out_ref[p] = (total + dot(theirs_ref[...], other_ref[p])).astype(BF16)


def sum_kernel(x_ref, out_ref):
    total = x_ref[0].astype(F32)
    for p in range(1, 4):
        total += x_ref[p].astype(F32)
    out_ref[...] = total.astype(BF16)


def regroup_pairs(j, rows, cross, groups):
    pairs = []
    for z in range(rows):
        for x in range(4):
            for y in range(groups):
                for c in range(2):
                    i = (x + j) % 2
                    pairs.append(((z * 4 + x) * cross + y * 2 + c, (z * 4 + 2 * c + i) * cross + y * 2 + x // 2))
    return pairs


def follow_pairs(rows, cross):
    pairs = []
    for b in range(4 * rows):
        for y in range(0, cross, 2):
            pairs.append((b * cross + y, b * cross + y + 1))
            if b + 4 < 4 * rows:
                pairs.append((b * cross + y + 1, (b + 4) * cross + y))
    return pairs


def return_groups(rows, cross):
    groups = []
    for z in range(rows):
        for y in range(0, cross, 2):
            for flip in (0, 1):
                groups.append([(z * 4 + x) * cross + y + (x // 2 ^ flip) for x in range(4)])
    return groups


def shape(dims, dtype=BF16):
    return jax.ShapeDtypeStruct(dims, dtype)


def shards(inputs, w_query, w_key, w_value, w_out, reflect_dir, strength, hop_count):
    both = ("ctx", "head")
    z = lax.axis_index("ctx") // 4
    x = lax.axis_index("ctx") % 4
    c = lax.axis_index("head") % 2
    at = jnp.stack([x % 2, c, 2 * z + c]).astype(jnp.int32)
    there = [regroup_pairs(j, 16, 8, 4) for j in range(2)]
    follow = follow_pairs(16, 8)
    down = [(b, b + 4) for b in range(60)]
    twin = [(h, h ^ 1) for h in range(8)]

    w, t, u, y, a = call(
        directions_kernel,
        [shape((2, TOK, DH)), shape((2, TOK, TOK)), shape((2, TOK, DH)), shape((2, TOK, DH)), shape((2, DH, DH))],
        2, flops=2**32,
    )(reflect_dir, strength)
    planes = [[0, 2, 4, 6], [1, 3, 5, 7]]
    copies = jnp.broadcast_to(inputs[None], (4, TOK, 256))
    gathered = lax.all_to_all(copies, "head", 0, 0, axis_index_groups=planes)
    other = lax.ppermute(gathered, "head", twin)
    halves = call(halves_kernel, shape((4, 256, 256)), 2, smem=1)(at, w_out)
    other_out = lax.ppermute(halves, "head", twin)
    p0, p1, q, k, v = call(
        project_kernel,
        [shape((PACK, DH)), shape((PACK, DH))] + [shape((2, TOK, DH))] * 3,
        11, smem=2, flops=2**30,
    )(at, hop_count, gathered, other, w_query, w_key, w_value, w, u, y, a)
    r0 = lax.ppermute(p0, both, there[0])
    r1 = lax.ppermute(p1, both, there[1])
    acc, lse = call(
        own_kernel, [shape((2, TOK, DH), F32), shape((2, TOK, DH), F32)], 5, flops=2**31
    )(q, k, v, w, t)
    qs, own_pair, hops = call(
        pair_kernel,
        [shape((3, 2, TOK, DH)), shape((PAIR, DH)), shape((2, 16, DH), F32)],
        3, smem=1, flops=2**28,
    )(at, r0, r1)
    d1 = lax.ppermute(own_pair, both, follow)
    d2 = lax.ppermute(own_pair, "ctx", down)
    d3 = lax.ppermute(d2, both, follow)
    d4 = lax.ppermute(d2, "ctx", down)
    state = [shape((2, TOK, DH), F32)] * 3 + [shape((2, TOK, DH))]
    near = call(near_kernel, state, 5, smem=1, flops=2**31)(at, qs, hops, d1, d2)
    far = call(far_kernel, shape((4, BACK, DH)), 8, smem=1, flops=2**30)(at, hops, d3, d4, *near)
    got = lax.all_to_all(far, both, 0, 0, axis_index_groups=return_groups(16, 8))
    mine = call(merge_kernel, shape((TOK, 2 * DH)), 4, smem=1, flops=2**28)(at, got, acc, lse)
    theirs = lax.ppermute(mine, "head", twin)
    partial = call(output_kernel, shape((4, TOK, 256)), 5, smem=1, flops=2**29)(
        at, mine, theirs, w_out, other_out
    )
    pieces = lax.all_to_all(partial, "head", 0, 0, axis_index_groups=planes)
    return call(sum_kernel, shape((TOK, 256)), 1)(pieces)


def solution(mesh):
    placed = (
        P("ctx", "head"),
        P(None, "head"),
        P(None, "head"),
        P(None, "head"),
        P("head", None),
        P("ctx", "head"),
        P("head", "ctx"),
        P("ctx"),
    )
    return jax.shard_map(
        shards, mesh=mesh, in_specs=placed, out_specs=P("ctx", "head"), check_vma=False
    )
```

```python
import jax
import jax.numpy as jnp
from jax import lax
from jax.experimental import pallas as pl
from jax.experimental.pallas import tpu as pltpu
from jax.sharding import PartitionSpec as P

TOK = 256
DH = 128
SCALE = 1.4426950408889634 / DH**0.5
NEG = -1e30
F32 = jnp.float32
BF16 = jnp.bfloat16
HOP_ROW = 3 * TOK + DH
PACK = HOP_ROW + 16
PAIR = 4 * TOK + DH
BACK = TOK + 16
VMEM = pl.BlockSpec(memory_space=pltpu.VMEM)
SMEM = pl.BlockSpec(memory_space=pltpu.SMEM)

NN = (((1,), (0,)), ((), ()))
NT = (((1,), (1,)), ((), ()))
TN = (((0,), (0,)), ((), ()))


def dot(a, b, dims=NN):
    return lax.dot_general(a, b, dims, preferred_element_type=F32)


def split(a):
    high = a.astype(BF16)
    return high, (a - high.astype(F32)).astype(BF16)


def exact(a, b):
    (ah, al), (bh, bl) = split(a), split(b)
    return dot(ah, bh) + (dot(ah, bl) + dot(al, bh))


def call(body, outs, ins, flops=0, smem=0, late=0):
    return pl.pallas_call(
        body,
        out_shape=outs,
        in_specs=[SMEM] * smem + [VMEM] * (ins - smem) + [pl.BlockSpec(memory_space=pl.ANY)] * late,
        out_specs=jax.tree.map(lambda _: VMEM, outs),
        compiler_params=pltpu.CompilerParams(vmem_limit_bytes=48 * 2**20),
        cost_estimate=pl.CostEstimate(flops=flops, bytes_accessed=2**20, transcendentals=0),
    )


def lower_inverses(blocks, row, col):
    eye = (row == col).astype(F32)
    same = (row // 4) == (col // 4)
    small = [jnp.where(same, b, 0.0) for b in blocks]
    squares = [exact(s, s) for s in small]
    found = [exact(eye - s, eye + q) for s, q in zip(small, squares)]
    size = 4
    while size < DH:
        off = ((row // (2 * size)) == (col // (2 * size))) & ((row // size) != (col // size))
        left = [exact(x, jnp.where(off, b, 0.0)) for x, b in zip(found, blocks)]
        found = [x - exact(y, x) for x, y in zip(found, left)]
        size *= 2
    return found


def directions_kernel(dirs_ref, beta_ref, w_ref, t_ref, u_ref, y_ref, a_ref, mark_ref):
    mark_ref[...] = jnp.zeros((8, DH), F32)
    row = lax.broadcasted_iota(jnp.int32, (TOK, TOK), 0)
    col = lax.broadcasted_iota(jnp.int32, (TOK, TOK), 1)
    strict = row > col
    r, c = row[:DH, :DH], col[:DH, :DH]
    dirs, lows, betas = [], [], []
    for h in range(2):
        d = dirs_ref[:, h * DH : (h + 1) * DH].astype(F32)
        d = d * lax.rsqrt(jnp.sum(d * d, axis=1, keepdims=True) + 1e-6)
        w = d.astype(BF16)
        dirs.append(w)
        beta = beta_ref[h : h + 1, :]
        column = jnp.sum(jnp.where(row == col, beta, 0.0), axis=1, keepdims=True)
        lows.append(jnp.where(strict, dot(w, w, NT) * column, 0.0))
        betas.append(beta)
    corners = []
    for low in lows:
        corners += [low[:DH, :DH], low[DH:, DH:]]
    found = lower_inverses(corners, r, c)
    for h in range(2):
        first, second = found[2 * h], found[2 * h + 1]
        cross = -exact(second, exact(lows[h][DH:, :DH], first))
        upper = jnp.concatenate([first, jnp.zeros((DH, DH), F32)], axis=1)
        lower = jnp.concatenate([cross, second], axis=1)
        t = (jnp.concatenate([upper, lower], axis=0) * betas[h]).astype(BF16)
        w = dirs[h]
        u = dot(t, w, TN).astype(BF16)
        w_ref[h] = w
        t_ref[h] = t
        u_ref[h] = u
        y_ref[h] = dot(t, w).astype(BF16)
        eye = (r == c).astype(F32)
        a_ref[h] = (eye - dot(u, w, TN)).astype(BF16)


def project_kernel(
    at_ref, hop_ref, x_ref, o_ref, wq_ref, wk_ref, wv_ref, w_ref, u_ref, y_ref, a_ref,
    mark_ref, p0_ref, p1_ref, q_ref, k_ref, v_ref,
):
    def product(weights):
        total = None
        for p in range(4):
            for ref, c in ((x_ref, at_ref[1]), (o_ref, 1 - at_ref[1])):
                rows = pl.ds(pl.multiple_of((2 * p + c) * 256, 256), 256)
                term = dot(ref[p], weights[rows, :])
                total = term if total is None else total + term
        return total.astype(BF16)

    del mark_ref
    query, key, value = product(wq_ref), product(wk_ref), product(wv_ref)
    for h in range(2):
        cut = slice(h * DH, (h + 1) * DH)
        q_ref[h] = query[:, cut]
        k_ref[h] = key[:, cut]
        v_ref[h] = value[:, cut]
    row = lax.broadcasted_iota(jnp.int32, (TOK, TOK), 0)
    col = lax.broadcasted_iota(jnp.int32, (TOK, TOK), 1)
    hops = hop_ref[0].astype(F32)
    for j, p_ref in enumerate((p0_ref, p1_ref)):
        h = lax.rem(at_ref[0] + j, 2)
        q, k, w = q_ref[h], k_ref[h], w_ref[h]
        qdirs = jnp.where(row >= col, dot(q, w, NT), 0.0).astype(BF16)
        keydirs = jnp.where(col > row, dot(k, w, NT), 0.0).astype(BF16)
        qhat = q.astype(F32) - dot(qdirs, y_ref[h])
        p_ref[0:TOK] = (qhat * SCALE).astype(BF16)
        p_ref[TOK : 2 * TOK] = (k.astype(F32) - dot(keydirs, u_ref[h])).astype(BF16)
        p_ref[2 * TOK : 3 * TOK] = v_ref[h]
        p_ref[3 * TOK : HOP_ROW] = a_ref[h]
        p_ref[HOP_ROW:PACK] = jnp.full((16, DH), hops, F32).astype(BF16)


def own_kernel(q_ref, k_ref, v_ref, w_ref, t_ref, acc_ref, lse_ref):
    row = lax.broadcasted_iota(jnp.int32, (TOK, TOK), 0)
    col = lax.broadcasted_iota(jnp.int32, (TOK, TOK), 1)
    for h in range(2):
        q, k, w = q_ref[h], k_ref[h], w_ref[h]
        qdirs = jnp.where(row >= col, dot(q, w, NT), 0.0).astype(BF16)
        dirkeys = jnp.where(row > col, dot(w, k, NT), 0.0).astype(BF16)
        coef = dot(qdirs, t_ref[h]).astype(BF16)
        own = (dot(q, k, NT) - dot(coef, dirkeys)) * SCALE
        own = jnp.where(row >= col, own, NEG)
        top = jnp.max(own, axis=1, keepdims=True)
        prob = jnp.exp2(own - top)
        total = jnp.sum(prob, axis=1, keepdims=True)
        acc_ref[h] = dot(prob.astype(BF16), v_ref[h]) / total
        lse_ref[h] = jnp.broadcast_to(top + jnp.log2(total), (TOK, DH))


def pair_kernel(at_ref, r0_ref, r1_ref, q_ref, pair_ref, hop_ref):
    swapped = at_ref[0] == 1

    def part(low, high):
        a, b = r0_ref[low:high], r1_ref[low:high]
        return jnp.where(swapped, b, a), jnp.where(swapped, a, b)

    q_even, q_odd = part(0, TOK)
    k_even, k_odd = part(TOK, 2 * TOK)
    v_even, v_odd = part(2 * TOK, 3 * TOK)
    a_even, a_odd = part(3 * TOK, HOP_ROW)
    h_even, h_odd = part(HOP_ROW, PACK)
    pair_ref[0:TOK] = dot(k_even, a_odd, NT).astype(BF16)
    pair_ref[TOK : 2 * TOK] = k_odd
    pair_ref[2 * TOK : 3 * TOK] = v_even
    pair_ref[3 * TOK : 4 * TOK] = v_odd
    pair_ref[4 * TOK : PAIR] = dot(a_odd, a_even).astype(BF16)
    q_ref[0, 0] = q_even
    q_ref[0, 1] = q_odd
    q_ref[1, 0] = q_even
    q_ref[1, 1] = dot(q_odd, a_even).astype(BF16)
    q_ref[2, 0] = k_even
    q_ref[2, 1] = v_even
    hop_ref[0] = h_even.astype(F32)
    hop_ref[1] = h_odd.astype(F32)


def window_step(q, keys, d, i, hops, pair):
    col = lax.broadcasted_iota(jnp.int32, (1, 2 * TOK), 1)
    distance = 2 * d + i - (col >= TOK).astype(jnp.int32)
    valid = (distance.astype(F32) <= hops) & (pair >= d)
    return dot(q, keys[0 : 2 * TOK], NT) + jnp.where(valid, 0.0, NEG)


def near_kernel(at_ref, q_ref, hop_ref, d1_ref, d2_ref, acc_ref, top_ref, total_ref, next_ref):
    pair = at_ref[2]
    for i in range(2):
        hops = hop_ref[i, 0:1, 0:1]
        q = q_ref[1, i]
        first = window_step(q, d1_ref, 1, i, hops, pair)
        q = dot(q, d1_ref[4 * TOK : PAIR]).astype(BF16)
        second = window_step(q, d2_ref, 2, i, hops, pair)
        next_ref[i] = dot(q, d2_ref[4 * TOK : PAIR]).astype(BF16)
        top = jnp.maximum(jnp.max(first, axis=1, keepdims=True), jnp.max(second, axis=1, keepdims=True))
        if i == 1:
            inside = dot(q_ref[0, 1], q_ref[2, 0], NT)
            top = jnp.maximum(top, jnp.max(inside, axis=1, keepdims=True))
        first, second = jnp.exp2(first - top), jnp.exp2(second - top)
        total = jnp.sum(first, axis=1, keepdims=True) + jnp.sum(second, axis=1, keepdims=True)
        acc = dot(first.astype(BF16), d1_ref[2 * TOK : 4 * TOK])
        acc += dot(second.astype(BF16), d2_ref[2 * TOK : 4 * TOK])
        if i == 1:
            inside = jnp.exp2(inside - top)
            total += jnp.sum(inside, axis=1, keepdims=True)
            acc += dot(inside.astype(BF16), q_ref[2, 1])
        acc_ref[i] = acc
        top_ref[i] = jnp.broadcast_to(top, (TOK, DH))
        total_ref[i] = jnp.broadcast_to(total, (TOK, DH))


def far_kernel(
    at_ref, hop_ref, d3_ref, d4_ref, acc_ref, top_ref, total_ref, next_ref, o0_ref, o1_ref
):
    pair = at_ref[2]
    for j, out_ref in enumerate((o0_ref, o1_ref)):
        i = lax.rem(at_ref[0] + j, 2)
        hops = hop_ref[i, 0:1, 0:1]
        q = next_ref[i]
        third = window_step(q, d3_ref, 3, i, hops, pair)
        q = dot(q, d3_ref[4 * TOK : PAIR]).astype(BF16)
        fourth = window_step(q, d4_ref, 4, i, hops, pair)
        before = top_ref[i, :, 0:1]
        top = jnp.maximum(jnp.max(third, axis=1, keepdims=True), jnp.max(fourth, axis=1, keepdims=True))
        top = jnp.maximum(top, before)
        third, fourth = jnp.exp2(third - top), jnp.exp2(fourth - top)
        kept = jnp.exp2(before - top)
        total = total_ref[i, :, 0:1] * kept
        total += jnp.sum(third, axis=1, keepdims=True) + jnp.sum(fourth, axis=1, keepdims=True)
        acc = acc_ref[i] * kept
        acc += dot(third.astype(BF16), d3_ref[2 * TOK : 4 * TOK])
        acc += dot(fourth.astype(BF16), d4_ref[2 * TOK : 4 * TOK])
        out_ref[0:TOK] = (acc / total).astype(BF16)
        lse = jnp.broadcast_to(top + jnp.log2(total), (TOK, DH)).T[0:16]
        high = lse.astype(BF16).astype(F32)
        low = lse - high
        line = lax.broadcasted_iota(jnp.int32, (16, DH), 0)
        tile = jnp.where(line == 0, high[:, :DH], high[:, DH:])
        tile = jnp.where(line == 2, low[:, :DH], tile)
        tile = jnp.where(line == 3, low[:, DH:], tile)
        out_ref[TOK:BACK] = tile.astype(BF16)


def merge_kernel(at_ref, g0_ref, g1_ref, acc_ref, lse_ref, out_ref):
    swapped = at_ref[0] == 1
    row = lax.broadcasted_iota(jnp.int32, (DH, DH), 0)
    col = lax.broadcasted_iota(jnp.int32, (DH, DH), 1)
    for h in range(2):
        a, b = (g0_ref, g1_ref) if h == 0 else (g1_ref, g0_ref)
        got = jnp.where(swapped, b[...], a[...]).astype(F32)
        tile = got[TOK:BACK]
        column = []
        for part in range(2):
            line = tile[part : part + 1] + tile[part + 2 : part + 3]
            column.append(jnp.sum(jnp.where(row == col, line, 0.0), axis=1, keepdims=True))
        far = jnp.concatenate(column, axis=0)
        own = lse_ref[h, :, 0:1]
        top = jnp.maximum(own, far)
        mine, theirs = jnp.exp2(own - top), jnp.exp2(far - top)
        mixed = (acc_ref[h] * mine + got[:TOK] * theirs) / (mine + theirs)
        out_ref[:, h * DH : (h + 1) * DH] = mixed.astype(BF16)


def columns(c, p):
    return pl.ds(pl.multiple_of((2 * p + c) * 256, 256), 256)


def halves_kernel(at_ref, wo_ref, out_ref):
    for p in range(4):
        out_ref[p] = wo_ref[:, columns(1 - at_ref[1], p)]


def output_kernel(at_ref, mine_ref, theirs_ref, wo_ref, other_ref, out_ref):
    for p in range(4):
        total = dot(mine_ref[...], wo_ref[:, columns(at_ref[1], p)])
        out_ref[p] = (total + dot(theirs_ref[...], other_ref[p])).astype(BF16)


def sum_kernel(x_ref, out_ref):
    total = x_ref[0].astype(F32)
    for p in range(1, 4):
        total += x_ref[p].astype(F32)
    out_ref[...] = total.astype(BF16)


def regroup_pairs(j, rows, cross, groups):
    pairs = []
    for z in range(rows):
        for x in range(4):
            for y in range(groups):
                for c in range(2):
                    i = (x + j) % 2
                    pairs.append(((z * 4 + x) * cross + y * 2 + c, (z * 4 + 2 * c + i) * cross + y * 2 + x // 2))
    return pairs


def follow_pairs(rows, cross):
    pairs = []
    for b in range(4 * rows):
        for y in range(0, cross, 2):
            pairs.append((b * cross + y, b * cross + y + 1))
            if b + 4 < 4 * rows:
                pairs.append((b * cross + y + 1, (b + 4) * cross + y))
    return pairs


def shape(dims, dtype=BF16):
    return jax.ShapeDtypeStruct(dims, dtype)


def shards(inputs, w_query, w_key, w_value, w_out, reflect_dir, strength, hop_count):
    both = ("ctx", "head")
    z = lax.axis_index("ctx") // 4
    x = lax.axis_index("ctx") % 4
    c = lax.axis_index("head") % 2
    at = jnp.stack([x % 2, c, 2 * z + c]).astype(jnp.int32)
    there = [regroup_pairs(j, 16, 8, 4) for j in range(2)]
    back = [[(b, a) for a, b in pairs] for pairs in there]
    follow = follow_pairs(16, 8)
    down = [(b, b + 4) for b in range(60)]
    twin = [(h, h ^ 1) for h in range(8)]

    w, t, u, y, a, mark = call(
        directions_kernel,
        [shape((2, TOK, DH)), shape((2, TOK, TOK)), shape((2, TOK, DH)), shape((2, TOK, DH)), shape((2, DH, DH)), shape((8, DH), F32)],
        2, flops=2**32,
    )(reflect_dir, strength)
    planes = [[0, 2, 4, 6], [1, 3, 5, 7]]
    copies = jnp.broadcast_to(inputs[None], (4, TOK, 256))
    gathered = lax.all_to_all(copies, "head", 0, 0, axis_index_groups=planes)
    gathered, mark = lax.optimization_barrier((gathered, mark))
    other = lax.ppermute(gathered, "head", twin)
    halves = call(halves_kernel, shape((4, 256, 256)), 2, smem=1)(at, w_out)
    other_out = lax.ppermute(halves, "head", twin)
    p0, p1, q, k, v = call(
        project_kernel,
        [shape((PACK, DH)), shape((PACK, DH))] + [shape((2, TOK, DH))] * 3,
        11, smem=2, flops=2**30, late=1,
    )(at, hop_count, gathered, other, w_query, w_key, w_value, w, u, y, a, mark)
    r0 = lax.ppermute(p0, both, there[0])
    r1 = lax.ppermute(p1, both, there[1])
    acc, lse = call(
        own_kernel, [shape((2, TOK, DH), F32), shape((2, TOK, DH), F32)], 5, flops=2**31
    )(q, k, v, w, t)
    qs, own_pair, hops = call(
        pair_kernel,
        [shape((3, 2, TOK, DH)), shape((PAIR, DH)), shape((2, 16, DH), F32)],
        3, smem=1, flops=2**28,
    )(at, r0, r1)
    d1 = lax.ppermute(own_pair, both, follow)
    d2 = lax.ppermute(own_pair, "ctx", down)
    d3 = lax.ppermute(d2, both, follow)
    d4 = lax.ppermute(d2, "ctx", down)
    state = [shape((2, TOK, DH), F32)] * 3 + [shape((2, TOK, DH))]
    near = call(near_kernel, state, 5, smem=1, flops=2**31)(at, qs, hops, d1, d2)
    o0, o1 = call(
        far_kernel, [shape((BACK, DH)), shape((BACK, DH))], 8, smem=1, flops=2**30
    )(at, hops, d3, d4, *near)
    g0 = lax.ppermute(o0, both, back[0])
    g1 = lax.ppermute(o1, both, back[1])
    mine = call(merge_kernel, shape((TOK, 2 * DH)), 5, smem=1, flops=2**28)(at, g0, g1, acc, lse)
    theirs = lax.ppermute(mine, "head", twin)
    partial = call(output_kernel, shape((4, TOK, 256)), 5, smem=1, flops=2**29)(
        at, mine, theirs, w_out, other_out
    )
    pieces = lax.all_to_all(partial, "head", 0, 0, axis_index_groups=planes)
    return call(sum_kernel, shape((TOK, 256)), 1)(pieces)


def solution(mesh):
    placed = (
        P("ctx", "head"),
        P(None, "head"),
        P(None, "head"),
        P(None, "head"),
        P("head", None),
        P("ctx", "head"),
        P("head", "ctx"),
        P("ctx"),
    )
    return jax.shard_map(
        shards, mesh=mesh, in_specs=placed, out_specs=P("ctx", "head"), check_vma=False
    )
```

```python
import jax
import jax.numpy as jnp
from jax import lax
from jax.experimental import pallas as pl
from jax.experimental.pallas import tpu as pltpu
from jax.sharding import PartitionSpec as P

TOK = 256
DH = 128
SCALE = 1.4426950408889634 / DH**0.5
NEG = -1e30
F32 = jnp.float32
BF16 = jnp.bfloat16
HOP_ROW = 3 * TOK + DH
PACK = HOP_ROW + 16
PAIR = 4 * TOK + DH
BACK = TOK + 16
VMEM = pl.BlockSpec(memory_space=pltpu.VMEM)
SMEM = pl.BlockSpec(memory_space=pltpu.SMEM)

NN = (((1,), (0,)), ((), ()))
NT = (((1,), (1,)), ((), ()))
TN = (((0,), (0,)), ((), ()))


def dot(a, b, dims=NN):
    return lax.dot_general(a, b, dims, preferred_element_type=F32)


def split(a):
    high = a.astype(BF16)
    return high, (a - high.astype(F32)).astype(BF16)


def exact(a, b):
    (ah, al), (bh, bl) = split(a), split(b)
    return dot(ah, bh) + (dot(ah, bl) + dot(al, bh))


def call(body, outs, ins, flops=0, smem=0, late=0):
    return pl.pallas_call(
        body,
        out_shape=outs,
        in_specs=[SMEM] * smem + [VMEM] * (ins - smem) + [pl.BlockSpec(memory_space=pl.ANY)] * late,
        out_specs=jax.tree.map(lambda _: VMEM, outs),
        compiler_params=pltpu.CompilerParams(vmem_limit_bytes=48 * 2**20),
        cost_estimate=pl.CostEstimate(flops=flops, bytes_accessed=2**20, transcendentals=0),
    )


def lower_inverses(blocks, row, col):
    eye = (row == col).astype(F32)
    same = (row // 4) == (col // 4)
    small = [jnp.where(same, b, 0.0) for b in blocks]
    squares = [exact(s, s) for s in small]
    found = [exact(eye - s, eye + q) for s, q in zip(small, squares)]
    size = 4
    while size < DH:
        off = ((row // (2 * size)) == (col // (2 * size))) & ((row // size) != (col // size))
        left = [exact(x, jnp.where(off, b, 0.0)) for x, b in zip(found, blocks)]
        found = [x - exact(y, x) for x, y in zip(found, left)]
        size *= 2
    return found


def directions_kernel(dirs_ref, beta_ref, w_ref, t_ref, mark_ref):
    mark_ref[...] = jnp.zeros((8, DH), F32)
    row = lax.broadcasted_iota(jnp.int32, (TOK, TOK), 0)
    col = lax.broadcasted_iota(jnp.int32, (TOK, TOK), 1)
    strict = row > col
    r, c = row[:DH, :DH], col[:DH, :DH]
    dirs, lows, betas = [], [], []
    for h in range(2):
        d = dirs_ref[:, h * DH : (h + 1) * DH].astype(F32)
        d = d * lax.rsqrt(jnp.sum(d * d, axis=1, keepdims=True) + 1e-6)
        w = d.astype(BF16)
        dirs.append(w)
        beta = beta_ref[h : h + 1, :]
        column = jnp.sum(jnp.where(row == col, beta, 0.0), axis=1, keepdims=True)
        lows.append(jnp.where(strict, dot(w, w, NT) * column, 0.0))
        betas.append(beta)
    corners = []
    for low in lows:
        corners += [low[:DH, :DH], low[DH:, DH:]]
    found = lower_inverses(corners, r, c)
    for h in range(2):
        first, second = found[2 * h], found[2 * h + 1]
        cross = -exact(second, exact(lows[h][DH:, :DH], first))
        upper = jnp.concatenate([first, jnp.zeros((DH, DH), F32)], axis=1)
        lower = jnp.concatenate([cross, second], axis=1)
        t = (jnp.concatenate([upper, lower], axis=0) * betas[h]).astype(BF16)
        w_ref[h] = dirs[h]
        t_ref[h] = t


def copies_kernel(x_ref, out_ref, sems):
    copies = [pltpu.make_async_copy(x_ref, out_ref.at[p], sems.at[p]) for p in range(4)]
    for copy in copies:
        copy.start()
    for copy in copies:
        copy.wait()


def project_kernel(
    at_ref, hop_ref, x_ref, o_ref, wq_ref, wk_ref, wv_ref, w_ref, t_ref,
    mark_ref, p0_ref, p1_ref, q_ref, k_ref, v_ref, c_ref,
):
    def product(weights):
        total = None
        for p in range(4):
            for ref, c in ((x_ref, at_ref[1]), (o_ref, 1 - at_ref[1])):
                rows = pl.ds(pl.multiple_of((2 * p + c) * 256, 256), 256)
                term = dot(ref[p], weights[rows, :])
                total = term if total is None else total + term
        return total.astype(BF16)

    del mark_ref
    query, key, value = product(wq_ref), product(wk_ref), product(wv_ref)
    for h in range(2):
        cut = slice(h * DH, (h + 1) * DH)
        q_ref[h] = query[:, cut]
        k_ref[h] = key[:, cut]
        v_ref[h] = value[:, cut]
    row = lax.broadcasted_iota(jnp.int32, (TOK, TOK), 0)
    col = lax.broadcasted_iota(jnp.int32, (TOK, TOK), 1)
    hops = hop_ref[0].astype(F32)
    eye = (row == col).astype(F32)[:DH, :DH]
    for j, p_ref in enumerate((p0_ref, p1_ref)):
        h = lax.rem(at_ref[0] + j, 2)
        q, k, w, t = q_ref[h], k_ref[h], w_ref[h], t_ref[h]
        u = dot(t, w, TN).astype(BF16)
        qdirs = jnp.where(row >= col, dot(q, w, NT), 0.0).astype(BF16)
        keydirs = jnp.where(col > row, dot(k, w, NT), 0.0).astype(BF16)
        coef = dot(qdirs, t).astype(BF16)
        c_ref[h] = coef
        qhat = q.astype(F32) - dot(coef, w)
        p_ref[0:TOK] = (qhat * SCALE).astype(BF16)
        p_ref[TOK : 2 * TOK] = (k.astype(F32) - dot(keydirs, u)).astype(BF16)
        p_ref[2 * TOK : 3 * TOK] = v_ref[h]
        p_ref[3 * TOK : HOP_ROW] = (eye - dot(u, w, TN)).astype(BF16)
        p_ref[HOP_ROW:PACK] = jnp.full((16, DH), hops, F32).astype(BF16)


def own_kernel(q_ref, k_ref, v_ref, w_ref, c_ref, acc_ref, lse_ref):
    row = lax.broadcasted_iota(jnp.int32, (TOK, TOK), 0)
    col = lax.broadcasted_iota(jnp.int32, (TOK, TOK), 1)
    for h in range(2):
        q, k, w = q_ref[h], k_ref[h], w_ref[h]
        dirkeys = jnp.where(row > col, dot(w, k, NT), 0.0).astype(BF16)
        own = (dot(q, k, NT) - dot(c_ref[h], dirkeys)) * SCALE
        own = jnp.where(row >= col, own, NEG)
        top = jnp.max(own, axis=1, keepdims=True)
        prob = jnp.exp2(own - top)
        total = jnp.sum(prob, axis=1, keepdims=True)
        acc_ref[h] = dot(prob.astype(BF16), v_ref[h]) / total
        lse_ref[h] = jnp.broadcast_to(top + jnp.log2(total), (TOK, DH))


def pair_kernel(at_ref, r0_ref, r1_ref, q_ref, pair_ref, hop_ref):
    swapped = at_ref[0] == 1

    def part(low, high):
        a, b = r0_ref[low:high], r1_ref[low:high]
        return jnp.where(swapped, b, a), jnp.where(swapped, a, b)

    q_even, q_odd = part(0, TOK)
    k_even, k_odd = part(TOK, 2 * TOK)
    v_even, v_odd = part(2 * TOK, 3 * TOK)
    a_even, a_odd = part(3 * TOK, HOP_ROW)
    h_even, h_odd = part(HOP_ROW, PACK)
    pair_ref[0:TOK] = dot(k_even, a_odd, NT).astype(BF16)
    pair_ref[TOK : 2 * TOK] = k_odd
    pair_ref[2 * TOK : 3 * TOK] = v_even
    pair_ref[3 * TOK : 4 * TOK] = v_odd
    pair_ref[4 * TOK : PAIR] = dot(a_odd, a_even).astype(BF16)
    q_ref[0, 0] = q_even
    q_ref[0, 1] = q_odd
    q_ref[1, 0] = q_even
    q_ref[1, 1] = dot(q_odd, a_even).astype(BF16)
    q_ref[2, 0] = k_even
    q_ref[2, 1] = v_even
    hop_ref[0] = h_even.astype(F32)
    hop_ref[1] = h_odd.astype(F32)


def window_step(q, keys, d, i, hops, pair):
    col = lax.broadcasted_iota(jnp.int32, (1, 2 * TOK), 1)
    distance = 2 * d + i - (col >= TOK).astype(jnp.int32)
    valid = (distance.astype(F32) <= hops) & (pair >= d)
    return dot(q, keys[0 : 2 * TOK], NT) + jnp.where(valid, 0.0, NEG)


def near_kernel(at_ref, q_ref, hop_ref, d1_ref, d2_ref, acc_ref, top_ref, total_ref, next_ref):
    pair = at_ref[2]
    for i in range(2):
        hops = hop_ref[i, 0:1, 0:1]
        q = q_ref[1, i]
        first = window_step(q, d1_ref, 1, i, hops, pair)
        q = dot(q, d1_ref[4 * TOK : PAIR]).astype(BF16)
        second = window_step(q, d2_ref, 2, i, hops, pair)
        next_ref[i] = dot(q, d2_ref[4 * TOK : PAIR]).astype(BF16)
        top = jnp.maximum(jnp.max(first, axis=1, keepdims=True), jnp.max(second, axis=1, keepdims=True))
        if i == 1:
            inside = dot(q_ref[0, 1], q_ref[2, 0], NT)
            top = jnp.maximum(top, jnp.max(inside, axis=1, keepdims=True))
        first, second = jnp.exp2(first - top), jnp.exp2(second - top)
        total = jnp.sum(first, axis=1, keepdims=True) + jnp.sum(second, axis=1, keepdims=True)
        acc = dot(first.astype(BF16), d1_ref[2 * TOK : 4 * TOK])
        acc += dot(second.astype(BF16), d2_ref[2 * TOK : 4 * TOK])
        if i == 1:
            inside = jnp.exp2(inside - top)
            total += jnp.sum(inside, axis=1, keepdims=True)
            acc += dot(inside.astype(BF16), q_ref[2, 1])
        acc_ref[i] = acc
        top_ref[i] = jnp.broadcast_to(top, (TOK, DH))
        total_ref[i] = jnp.broadcast_to(total, (TOK, DH))


def far_kernel(
    at_ref, hop_ref, d3_ref, d4_ref, acc_ref, top_ref, total_ref, next_ref, o0_ref, o1_ref
):
    pair = at_ref[2]
    for j, out_ref in enumerate((o0_ref, o1_ref)):
        i = lax.rem(at_ref[0] + j, 2)
        hops = hop_ref[i, 0:1, 0:1]
        q = next_ref[i]
        third = window_step(q, d3_ref, 3, i, hops, pair)
        q = dot(q, d3_ref[4 * TOK : PAIR]).astype(BF16)
        fourth = window_step(q, d4_ref, 4, i, hops, pair)
        before = top_ref[i, :, 0:1]
        top = jnp.maximum(jnp.max(third, axis=1, keepdims=True), jnp.max(fourth, axis=1, keepdims=True))
        top = jnp.maximum(top, before)
        third, fourth = jnp.exp2(third - top), jnp.exp2(fourth - top)
        kept = jnp.exp2(before - top)
        total = total_ref[i, :, 0:1] * kept
        total += jnp.sum(third, axis=1, keepdims=True) + jnp.sum(fourth, axis=1, keepdims=True)
        acc = acc_ref[i] * kept
        acc += dot(third.astype(BF16), d3_ref[2 * TOK : 4 * TOK])
        acc += dot(fourth.astype(BF16), d4_ref[2 * TOK : 4 * TOK])
        out_ref[0:TOK] = (acc / total).astype(BF16)
        lse = jnp.broadcast_to(top + jnp.log2(total), (TOK, DH)).T[0:16]
        high = lse.astype(BF16).astype(F32)
        low = lse - high
        line = lax.broadcasted_iota(jnp.int32, (16, DH), 0)
        tile = jnp.where(line == 0, high[:, :DH], high[:, DH:])
        tile = jnp.where(line == 2, low[:, :DH], tile)
        tile = jnp.where(line == 3, low[:, DH:], tile)
        out_ref[TOK:BACK] = tile.astype(BF16)


def merge_kernel(at_ref, g0_ref, g1_ref, acc_ref, lse_ref, out_ref):
    swapped = at_ref[0] == 1
    row = lax.broadcasted_iota(jnp.int32, (DH, DH), 0)
    col = lax.broadcasted_iota(jnp.int32, (DH, DH), 1)
    for h in range(2):
        a, b = (g0_ref, g1_ref) if h == 0 else (g1_ref, g0_ref)
        got = jnp.where(swapped, b[...], a[...]).astype(F32)
        tile = got[TOK:BACK]
        column = []
        for part in range(2):
            line = tile[part : part + 1] + tile[part + 2 : part + 3]
            column.append(jnp.sum(jnp.where(row == col, line, 0.0), axis=1, keepdims=True))
        far = jnp.concatenate(column, axis=0)
        own = lse_ref[h, :, 0:1]
        top = jnp.maximum(own, far)
        mine, theirs = jnp.exp2(own - top), jnp.exp2(far - top)
        mixed = (acc_ref[h] * mine + got[:TOK] * theirs) / (mine + theirs)
        out_ref[:, h * DH : (h + 1) * DH] = mixed.astype(BF16)


def columns(c, p):
    return pl.ds(pl.multiple_of((2 * p + c) * 256, 256), 256)


def halves_kernel(at_ref, wo_ref, out_ref):
    for p in range(4):
        out_ref[p] = wo_ref[:, columns(1 - at_ref[1], p)]


def output_kernel(at_ref, mine_ref, theirs_ref, wo_ref, other_ref, out_ref):
    for p in range(4):
        total = dot(mine_ref[...], wo_ref[:, columns(at_ref[1], p)])
        out_ref[p] = (total + dot(theirs_ref[...], other_ref[p])).astype(BF16)


def sum_kernel(x_ref, out_ref):
    total = x_ref[0].astype(F32)
    for p in range(1, 4):
        total += x_ref[p].astype(F32)
    out_ref[...] = total.astype(BF16)


def regroup_pairs(j, rows, cross, groups):
    pairs = []
    for z in range(rows):
        for x in range(4):
            for y in range(groups):
                for c in range(2):
                    i = (x + j) % 2
                    pairs.append(((z * 4 + x) * cross + y * 2 + c, (z * 4 + 2 * c + i) * cross + y * 2 + x // 2))
    return pairs


def follow_pairs(rows, cross):
    pairs = []
    for b in range(4 * rows):
        for y in range(0, cross, 2):
            pairs.append((b * cross + y, b * cross + y + 1))
            if b + 4 < 4 * rows:
                pairs.append((b * cross + y + 1, (b + 4) * cross + y))
    return pairs


def shape(dims, dtype=BF16):
    return jax.ShapeDtypeStruct(dims, dtype)


def shards(inputs, w_query, w_key, w_value, w_out, reflect_dir, strength, hop_count):
    both = ("ctx", "head")
    z = lax.axis_index("ctx") // 4
    x = lax.axis_index("ctx") % 4
    c = lax.axis_index("head") % 2
    at = jnp.stack([x % 2, c, 2 * z + c]).astype(jnp.int32)
    there = [regroup_pairs(j, 16, 8, 4) for j in range(2)]
    back = [[(b, a) for a, b in pairs] for pairs in there]
    follow = follow_pairs(16, 8)
    down = [(b, b + 4) for b in range(60)]
    twin = [(h, h ^ 1) for h in range(8)]

    w, t, mark = call(
        directions_kernel, [shape((2, TOK, DH)), shape((2, TOK, TOK)), shape((8, DH), F32)], 2, flops=2**32
    )(reflect_dir, strength)
    planes = [[0, 2, 4, 6], [1, 3, 5, 7]]
    copies = pl.pallas_call(
        copies_kernel,
        out_shape=shape((4, TOK, 256)),
        in_specs=[pl.BlockSpec(memory_space=pl.ANY)],
        out_specs=pl.BlockSpec(memory_space=pl.ANY),
        scratch_shapes=[pltpu.SemaphoreType.DMA((4,))],
        compiler_params=pltpu.CompilerParams(vmem_limit_bytes=62 * 2**20),
        cost_estimate=pl.CostEstimate(flops=0, bytes_accessed=2**20, transcendentals=0),
    )(inputs)
    gathered = lax.all_to_all(copies, "head", 0, 0, axis_index_groups=planes)
    gathered, mark = lax.optimization_barrier((gathered, mark))
    other = lax.ppermute(gathered, "head", twin)
    halves = call(halves_kernel, shape((4, 256, 256)), 2, smem=1)(at, w_out)
    other_out = lax.ppermute(halves, "head", twin)
    p0, p1, q, k, v, coef = call(
        project_kernel,
        [shape((PACK, DH)), shape((PACK, DH))] + [shape((2, TOK, DH))] * 3 + [shape((2, TOK, TOK))],
        9, smem=2, flops=2**30, late=1,
    )(at, hop_count, gathered, other, w_query, w_key, w_value, w, t, mark)
    r0 = lax.ppermute(p0, both, there[0])
    r1 = lax.ppermute(p1, both, there[1])
    acc, lse = call(
        own_kernel, [shape((2, TOK, DH), F32), shape((2, TOK, DH), F32)], 5, flops=2**31
    )(q, k, v, w, coef)
    qs, own_pair, hops = call(
        pair_kernel,
        [shape((3, 2, TOK, DH)), shape((PAIR, DH)), shape((2, 16, DH), F32)],
        3, smem=1, flops=2**28,
    )(at, r0, r1)
    d1 = lax.ppermute(own_pair, both, follow)
    d2 = lax.ppermute(own_pair, "ctx", down)
    d3 = lax.ppermute(d2, both, follow)
    d4 = lax.ppermute(d2, "ctx", down)
    state = [shape((2, TOK, DH), F32)] * 3 + [shape((2, TOK, DH))]
    near = call(near_kernel, state, 5, smem=1, flops=2**31)(at, qs, hops, d1, d2)
    o0, o1 = call(
        far_kernel, [shape((BACK, DH)), shape((BACK, DH))], 8, smem=1, flops=2**30
    )(at, hops, d3, d4, *near)
    g0 = lax.ppermute(o0, both, back[0])
    g1 = lax.ppermute(o1, both, back[1])
    mine = call(merge_kernel, shape((TOK, 2 * DH)), 5, smem=1, flops=2**28)(at, g0, g1, acc, lse)
    theirs = lax.ppermute(mine, "head", twin)
    partial = call(output_kernel, shape((4, TOK, 256)), 5, smem=1, flops=2**29)(
        at, mine, theirs, w_out, other_out
    )
    pieces = lax.all_to_all(partial, "head", 0, 0, axis_index_groups=planes)
    return call(sum_kernel, shape((TOK, 256)), 1)(pieces)


def solution(mesh):
    placed = (
        P("ctx", "head"),
        P(None, "head"),
        P(None, "head"),
        P(None, "head"),
        P("head", None),
        P("ctx", "head"),
        P("head", "ctx"),
        P("ctx"),
    )
    return jax.shard_map(
        shards, mesh=mesh, in_specs=placed, out_specs=P("ctx", "head"), check_vma=False
    )
```

```python
import jax
import jax.numpy as jnp
from jax import lax
from jax.experimental import pallas as pl
from jax.experimental.pallas import tpu as pltpu
from jax.sharding import PartitionSpec as P

TOK = 256
DH = 128
SCALE = 1.4426950408889634 / DH**0.5
NEG = -1e30
F32 = jnp.float32
BF16 = jnp.bfloat16
HOP_ROW = 3 * TOK + DH
PACK = HOP_ROW + 16
PAIR = 4 * TOK + DH
BACK = TOK + 16
VMEM = pl.BlockSpec(memory_space=pltpu.VMEM)
SMEM = pl.BlockSpec(memory_space=pltpu.SMEM)

NN = (((1,), (0,)), ((), ()))
NT = (((1,), (1,)), ((), ()))
TN = (((0,), (0,)), ((), ()))


def dot(a, b, dims=NN):
    return lax.dot_general(a, b, dims, preferred_element_type=F32)


def split(a):
    high = a.astype(BF16)
    return high, (a - high.astype(F32)).astype(BF16)


def exact(a, b):
    (ah, al), (bh, bl) = split(a), split(b)
    return dot(ah, bh) + (dot(ah, bl) + dot(al, bh))


def call(body, outs, ins, flops=0, smem=0, late=0, scratch=()):
    return pl.pallas_call(
        body,
        out_shape=outs,
        in_specs=[SMEM] * smem + [VMEM] * (ins - smem) + [pl.BlockSpec(memory_space=pl.ANY)] * late,
        out_specs=jax.tree.map(lambda _: VMEM, outs),
        scratch_shapes=list(scratch),
        compiler_params=pltpu.CompilerParams(vmem_limit_bytes=48 * 2**20),
        cost_estimate=pl.CostEstimate(flops=flops, bytes_accessed=2**20, transcendentals=0),
    )


def lower_inverses(blocks, row, col):
    eye = (row == col).astype(F32)
    same = (row // 4) == (col // 4)
    small = [jnp.where(same, b, 0.0) for b in blocks]
    squares = [exact(s, s) for s in small]
    found = [exact(eye - s, eye + q) for s, q in zip(small, squares)]
    size = 4
    while size < DH:
        off = ((row // (2 * size)) == (col // (2 * size))) & ((row // size) != (col // size))
        left = [exact(x, jnp.where(off, b, 0.0)) for x, b in zip(found, blocks)]
        found = [x - exact(y, x) for x, y in zip(found, left)]
        size *= 2
    return found


def directions_kernel(dirs_ref, beta_ref, w_ref, t_ref, mark_ref):
    mark_ref[...] = jnp.zeros((8, DH), F32)
    row = lax.broadcasted_iota(jnp.int32, (TOK, TOK), 0)
    col = lax.broadcasted_iota(jnp.int32, (TOK, TOK), 1)
    strict = row > col
    r, c = row[:DH, :DH], col[:DH, :DH]
    dirs, lows, betas = [], [], []
    for h in range(2):
        d = dirs_ref[:, h * DH : (h + 1) * DH].astype(F32)
        d = d * lax.rsqrt(jnp.sum(d * d, axis=1, keepdims=True) + 1e-6)
        w = d.astype(BF16)
        dirs.append(w)
        beta = beta_ref[h : h + 1, :]
        column = jnp.sum(jnp.where(row == col, beta, 0.0), axis=1, keepdims=True)
        lows.append(jnp.where(strict, dot(w, w, NT) * column, 0.0))
        betas.append(beta)
    corners = []
    for low in lows:
        corners += [low[:DH, :DH], low[DH:, DH:]]
    found = lower_inverses(corners, r, c)
    for h in range(2):
        first, second = found[2 * h], found[2 * h + 1]
        cross = -exact(second, exact(lows[h][DH:, :DH], first))
        upper = jnp.concatenate([first, jnp.zeros((DH, DH), F32)], axis=1)
        lower = jnp.concatenate([cross, second], axis=1)
        t = (jnp.concatenate([upper, lower], axis=0) * betas[h]).astype(BF16)
        w_ref[h] = dirs[h]
        t_ref[h] = t


def project_kernel(
    at_ref, hop_ref, x_ref, o_ref, wq_ref, wk_ref, wv_ref, w_ref, t_ref,
    mark_ref, p0_ref, p1_ref, q_ref, k_ref, v_ref, c_ref, rows_ref,
):
    del mark_ref
    for p in range(4):
        rows_ref[:, columns(at_ref[1], p)] = x_ref[p]
        rows_ref[:, columns(1 - at_ref[1], p)] = o_ref[p]
    rows = rows_ref[...]
    query, key, value = (dot(rows, ref[...]).astype(BF16) for ref in (wq_ref, wk_ref, wv_ref))
    for h in range(2):
        cut = slice(h * DH, (h + 1) * DH)
        q_ref[h] = query[:, cut]
        k_ref[h] = key[:, cut]
        v_ref[h] = value[:, cut]
    row = lax.broadcasted_iota(jnp.int32, (TOK, TOK), 0)
    col = lax.broadcasted_iota(jnp.int32, (TOK, TOK), 1)
    hops = hop_ref[0].astype(F32)
    eye = (row == col).astype(F32)[:DH, :DH]
    for j, p_ref in enumerate((p0_ref, p1_ref)):
        h = lax.rem(at_ref[0] + j, 2)
        q, k, w, t = q_ref[h], k_ref[h], w_ref[h], t_ref[h]
        u = dot(t, w, TN).astype(BF16)
        qdirs = jnp.where(row >= col, dot(q, w, NT), 0.0).astype(BF16)
        keydirs = jnp.where(col > row, dot(k, w, NT), 0.0).astype(BF16)
        coef = dot(qdirs, t).astype(BF16)
        c_ref[h] = coef
        qhat = q.astype(F32) - dot(coef, w)
        p_ref[0:TOK] = (qhat * SCALE).astype(BF16)
        p_ref[TOK : 2 * TOK] = (k.astype(F32) - dot(keydirs, u)).astype(BF16)
        p_ref[2 * TOK : 3 * TOK] = v_ref[h]
        p_ref[3 * TOK : HOP_ROW] = (eye - dot(u, w, TN)).astype(BF16)
        p_ref[HOP_ROW:PACK] = jnp.full((16, DH), hops, F32).astype(BF16)


def own_kernel(q_ref, k_ref, v_ref, w_ref, c_ref, acc_ref, lse_ref):
    row = lax.broadcasted_iota(jnp.int32, (TOK, TOK), 0)
    col = lax.broadcasted_iota(jnp.int32, (TOK, TOK), 1)
    for h in range(2):
        q, k, w = q_ref[h], k_ref[h], w_ref[h]
        dirkeys = jnp.where(row > col, dot(w, k, NT), 0.0).astype(BF16)
        own = (dot(q, k, NT) - dot(c_ref[h], dirkeys)) * SCALE
        own = jnp.where(row >= col, own, NEG)
        top = jnp.max(own, axis=1, keepdims=True)
        prob = jnp.exp2(own - top)
        total = jnp.sum(prob, axis=1, keepdims=True)
        acc_ref[h] = dot(prob.astype(BF16), v_ref[h]) / total
        lse_ref[h] = jnp.broadcast_to(top + jnp.log2(total), (TOK, DH))


def pair_kernel(at_ref, r0_ref, r1_ref, q_ref, pair_ref, hop_ref):
    swapped = at_ref[0] == 1

    def part(low, high):
        a, b = r0_ref[low:high], r1_ref[low:high]
        return jnp.where(swapped, b, a), jnp.where(swapped, a, b)

    q_even, q_odd = part(0, TOK)
    k_even, k_odd = part(TOK, 2 * TOK)
    v_even, v_odd = part(2 * TOK, 3 * TOK)
    a_even, a_odd = part(3 * TOK, HOP_ROW)
    h_even, h_odd = part(HOP_ROW, PACK)
    pair_ref[0:TOK] = dot(k_even, a_odd, NT).astype(BF16)
    pair_ref[TOK : 2 * TOK] = k_odd
    pair_ref[2 * TOK : 3 * TOK] = v_even
    pair_ref[3 * TOK : 4 * TOK] = v_odd
    pair_ref[4 * TOK : PAIR] = dot(a_odd, a_even).astype(BF16)
    q_ref[0, 0] = q_even
    q_ref[0, 1] = q_odd
    q_ref[1, 0] = q_even
    q_ref[1, 1] = dot(q_odd, a_even).astype(BF16)
    q_ref[2, 0] = k_even
    q_ref[2, 1] = v_even
    hop_ref[0] = h_even.astype(F32)
    hop_ref[1] = h_odd.astype(F32)


def window_step(q, keys, d, i, hops, pair):
    col = lax.broadcasted_iota(jnp.int32, (1, 2 * TOK), 1)
    distance = 2 * d + i - (col >= TOK).astype(jnp.int32)
    valid = (distance.astype(F32) <= hops) & (pair >= d)
    return dot(q, keys[0 : 2 * TOK], NT) + jnp.where(valid, 0.0, NEG)


def near_kernel(at_ref, q_ref, hop_ref, d1_ref, d2_ref, acc_ref, top_ref, total_ref, next_ref):
    pair = at_ref[2]
    for i in range(2):
        hops = hop_ref[i, 0:1, 0:1]
        q = q_ref[1, i]
        first = window_step(q, d1_ref, 1, i, hops, pair)
        q = dot(q, d1_ref[4 * TOK : PAIR]).astype(BF16)
        second = window_step(q, d2_ref, 2, i, hops, pair)
        next_ref[i] = dot(q, d2_ref[4 * TOK : PAIR]).astype(BF16)
        top = jnp.max(jnp.maximum(first, second), axis=1, keepdims=True)
        if i == 1:
            inside = dot(q_ref[0, 1], q_ref[2, 0], NT)
            top = jnp.maximum(top, jnp.max(inside, axis=1, keepdims=True))
        first, second = jnp.exp2(first - top), jnp.exp2(second - top)
        total = jnp.sum(first + second, axis=1, keepdims=True)
        acc = dot(first.astype(BF16), d1_ref[2 * TOK : 4 * TOK])
        acc += dot(second.astype(BF16), d2_ref[2 * TOK : 4 * TOK])
        if i == 1:
            inside = jnp.exp2(inside - top)
            total += jnp.sum(inside, axis=1, keepdims=True)
            acc += dot(inside.astype(BF16), q_ref[2, 1])
        acc_ref[i] = acc
        top_ref[i] = jnp.broadcast_to(top, (TOK, DH))
        total_ref[i] = jnp.broadcast_to(total, (TOK, DH))


def far_kernel(
    at_ref, hop_ref, d3_ref, d4_ref, acc_ref, top_ref, total_ref, next_ref, o0_ref, o1_ref
):
    pair = at_ref[2]
    for j, out_ref in enumerate((o0_ref, o1_ref)):
        i = lax.rem(at_ref[0] + j, 2)
        hops = hop_ref[i, 0:1, 0:1]
        q = next_ref[i]
        third = window_step(q, d3_ref, 3, i, hops, pair)
        q = dot(q, d3_ref[4 * TOK : PAIR]).astype(BF16)
        fourth = window_step(q, d4_ref, 4, i, hops, pair)
        before = top_ref[i, :, 0:1]
        top = jnp.maximum(jnp.max(jnp.maximum(third, fourth), axis=1, keepdims=True), before)
        third, fourth = jnp.exp2(third - top), jnp.exp2(fourth - top)
        kept = jnp.exp2(before - top)
        total = total_ref[i, :, 0:1] * kept
        total += jnp.sum(third + fourth, axis=1, keepdims=True)
        acc = acc_ref[i] * kept
        acc += dot(third.astype(BF16), d3_ref[2 * TOK : 4 * TOK])
        acc += dot(fourth.astype(BF16), d4_ref[2 * TOK : 4 * TOK])
        out_ref[0:TOK] = (acc / total).astype(BF16)
        lse = jnp.broadcast_to(top + jnp.log2(total), (TOK, DH)).T[0:16]
        high = lse.astype(BF16).astype(F32)
        low = lse - high
        line = lax.broadcasted_iota(jnp.int32, (16, DH), 0)
        tile = jnp.where(line == 0, high[:, :DH], high[:, DH:])
        tile = jnp.where(line == 2, low[:, :DH], tile)
        tile = jnp.where(line == 3, low[:, DH:], tile)
        out_ref[TOK:BACK] = tile.astype(BF16)


def merge_kernel(at_ref, g0_ref, g1_ref, acc_ref, lse_ref, out_ref):
    swapped = at_ref[0] == 1
    row = lax.broadcasted_iota(jnp.int32, (DH, DH), 0)
    col = lax.broadcasted_iota(jnp.int32, (DH, DH), 1)
    for h in range(2):
        a, b = (g0_ref, g1_ref) if h == 0 else (g1_ref, g0_ref)
        got = jnp.where(swapped, b[...], a[...]).astype(F32)
        tile = got[TOK:BACK]
        column = []
        for part in range(2):
            line = tile[part : part + 1] + tile[part + 2 : part + 3]
            column.append(jnp.sum(jnp.where(row == col, line, 0.0), axis=1, keepdims=True))
        far = jnp.concatenate(column, axis=0)
        own = lse_ref[h, :, 0:1]
        top = jnp.maximum(own, far)
        mine, theirs = jnp.exp2(own - top), jnp.exp2(far - top)
        mixed = (acc_ref[h] * mine + got[:TOK] * theirs) / (mine + theirs)
        out_ref[:, h * DH : (h + 1) * DH] = mixed.astype(BF16)


def columns(c, p):
    return pl.ds(pl.multiple_of((2 * p + c) * 256, 256), 256)


def halves_kernel(at_ref, wo_ref, out_ref):
    for p in range(4):
        out_ref[p] = wo_ref[:, columns(1 - at_ref[1], p)]


def output_kernel(at_ref, mine_ref, theirs_ref, wo_ref, other_ref, out_ref):
    for p in range(4):
        total = dot(mine_ref[...], wo_ref[:, columns(at_ref[1], p)])
        out_ref[p] = (total + dot(theirs_ref[...], other_ref[p])).astype(BF16)


def sum_kernel(x_ref, out_ref):
    total = x_ref[0].astype(F32)
    for p in range(1, 4):
        total += x_ref[p].astype(F32)
    out_ref[...] = total.astype(BF16)


def regroup_pairs(j, rows, cross, groups):
    pairs = []
    for z in range(rows):
        for x in range(4):
            for y in range(groups):
                for c in range(2):
                    i = (x + j) % 2
                    pairs.append(((z * 4 + x) * cross + y * 2 + c, (z * 4 + 2 * c + i) * cross + y * 2 + x // 2))
    return pairs


def follow_pairs(rows, cross):
    pairs = []
    for b in range(4 * rows):
        for y in range(0, cross, 2):
            pairs.append((b * cross + y, b * cross + y + 1))
            if b + 4 < 4 * rows:
                pairs.append((b * cross + y + 1, (b + 4) * cross + y))
    return pairs


def shape(dims, dtype=BF16):
    return jax.ShapeDtypeStruct(dims, dtype)


def shards(inputs, w_query, w_key, w_value, w_out, reflect_dir, strength, hop_count):
    both = ("ctx", "head")
    z = lax.axis_index("ctx") // 4
    x = lax.axis_index("ctx") % 4
    c = lax.axis_index("head") % 2
    at = jnp.stack([x % 2, c, 2 * z + c]).astype(jnp.int32)
    there = [regroup_pairs(j, 16, 8, 4) for j in range(2)]
    back = [[(b, a) for a, b in pairs] for pairs in there]
    follow = follow_pairs(16, 8)
    down = [(b, b + 4) for b in range(60)]
    twin = [(h, h ^ 1) for h in range(8)]

    w, t, mark = call(
        directions_kernel, [shape((2, TOK, DH)), shape((2, TOK, TOK)), shape((8, DH), F32)], 2, flops=2**32
    )(reflect_dir, strength)
    planes = [[0, 2, 4, 6], [1, 3, 5, 7]]
    copies = jnp.broadcast_to(inputs[None], (4, TOK, 256))
    gathered = lax.all_to_all(copies, "head", 0, 0, axis_index_groups=planes)
    gathered, mark = lax.optimization_barrier((gathered, mark))
    other = lax.ppermute(gathered, "head", twin)
    halves = call(halves_kernel, shape((4, 256, 256)), 2, smem=1)(at, w_out)
    other_out = lax.ppermute(halves, "head", twin)
    p0, p1, q, k, v, coef = call(
        project_kernel,
        [shape((PACK, DH)), shape((PACK, DH))] + [shape((2, TOK, DH))] * 3 + [shape((2, TOK, TOK))],
        9, smem=2, flops=2**30, late=1, scratch=[pltpu.VMEM((TOK, 2048), BF16)],
    )(at, hop_count, gathered, other, w_query, w_key, w_value, w, t, mark)
    r0 = lax.ppermute(p0, both, there[0])
    r1 = lax.ppermute(p1, both, there[1])
    acc, lse = call(
        own_kernel, [shape((2, TOK, DH), F32), shape((2, TOK, DH), F32)], 5, flops=2**31
    )(q, k, v, w, coef)
    qs, own_pair, hops = call(
        pair_kernel,
        [shape((3, 2, TOK, DH)), shape((PAIR, DH)), shape((2, 16, DH), F32)],
        3, smem=1, flops=2**28,
    )(at, r0, r1)
    d1 = lax.ppermute(own_pair, both, follow)
    d2 = lax.ppermute(own_pair, "ctx", down)
    d3 = lax.ppermute(d2, both, follow)
    d4 = lax.ppermute(d2, "ctx", down)
    state = [shape((2, TOK, DH), F32)] * 3 + [shape((2, TOK, DH))]
    near = call(near_kernel, state, 5, smem=1, flops=2**31)(at, qs, hops, d1, d2)
    o0, o1 = call(
        far_kernel, [shape((BACK, DH)), shape((BACK, DH))], 8, smem=1, flops=2**30
    )(at, hops, d3, d4, *near)
    g0 = lax.ppermute(o0, both, back[0])
    g1 = lax.ppermute(o1, both, back[1])
    mine = call(merge_kernel, shape((TOK, 2 * DH)), 5, smem=1, flops=2**28)(at, g0, g1, acc, lse)
    theirs = lax.ppermute(mine, "head", twin)
    partial = call(output_kernel, shape((4, TOK, 256)), 5, smem=1, flops=2**29)(
        at, mine, theirs, w_out, other_out
    )
    pieces = lax.all_to_all(partial, "head", 0, 0, axis_index_groups=planes)
    return call(sum_kernel, shape((TOK, 256)), 1)(pieces)


def solution(mesh):
    placed = (
        P("ctx", "head"),
        P(None, "head"),
        P(None, "head"),
        P(None, "head"),
        P("head", None),
        P("ctx", "head"),
        P("head", "ctx"),
        P("ctx"),
    )
    return jax.shard_map(
        shards, mesh=mesh, in_specs=placed, out_specs=P("ctx", "head"), check_vma=False
    )
```

```python
import jax
import jax.numpy as jnp
from jax import lax
from jax.experimental import pallas as pl
from jax.experimental.pallas import tpu as pltpu
from jax.sharding import PartitionSpec as P

TOK = 256
DH = 128
SCALE = 1.4426950408889634 / DH**0.5
NEG = -1e30
F32 = jnp.float32
BF16 = jnp.bfloat16
HOP_ROW = 3 * TOK + DH
PACK = HOP_ROW + 16
PAIR = 4 * TOK + DH
BACK = TOK + 16
VMEM = pl.BlockSpec(memory_space=pltpu.VMEM)
SMEM = pl.BlockSpec(memory_space=pltpu.SMEM)

NN = (((1,), (0,)), ((), ()))
NT = (((1,), (1,)), ((), ()))
TN = (((0,), (0,)), ((), ()))


def dot(a, b, dims=NN):
    return lax.dot_general(a, b, dims, preferred_element_type=F32)


def split(a):
    high = a.astype(BF16)
    return high, (a - high.astype(F32)).astype(BF16)


def exact(a, b):
    (ah, al), (bh, bl) = split(a), split(b)
    return dot(ah, bh) + (dot(ah, bl) + dot(al, bh))


def call(body, outs, ins, flops=0, smem=0, late=0, scratch=()):
    return pl.pallas_call(
        body,
        out_shape=outs,
        in_specs=[SMEM] * smem + [VMEM] * (ins - smem) + [pl.BlockSpec(memory_space=pl.ANY)] * late,
        out_specs=jax.tree.map(lambda _: VMEM, outs),
        scratch_shapes=list(scratch),
        compiler_params=pltpu.CompilerParams(vmem_limit_bytes=48 * 2**20),
        cost_estimate=pl.CostEstimate(flops=flops, bytes_accessed=2**20, transcendentals=0),
    )


def lower_inverses(blocks, row, col):
    eye = (row == col).astype(F32)
    same = (row // 4) == (col // 4)
    small = [jnp.where(same, b, 0.0) for b in blocks]
    squares = [exact(s, s) for s in small]
    found = [exact(eye - s, eye + q) for s, q in zip(small, squares)]
    size = 4
    while size < DH:
        off = ((row // (2 * size)) == (col // (2 * size))) & ((row // size) != (col // size))
        left = [exact(x, jnp.where(off, b, 0.0)) for x, b in zip(found, blocks)]
        found = [x - exact(y, x) for x, y in zip(found, left)]
        size *= 2
    return found


def directions_kernel(dirs_ref, beta_ref, w_ref, t_ref, mark_ref):
    mark_ref[...] = jnp.zeros((8, DH), F32)
    row = lax.broadcasted_iota(jnp.int32, (TOK, TOK), 0)
    col = lax.broadcasted_iota(jnp.int32, (TOK, TOK), 1)
    strict = row > col
    r, c = row[:DH, :DH], col[:DH, :DH]
    dirs, lows, betas = [], [], []
    for h in range(2):
        d = dirs_ref[:, h * DH : (h + 1) * DH].astype(F32)
        d = d * lax.rsqrt(jnp.sum(d * d, axis=1, keepdims=True) + 1e-6)
        w = d.astype(BF16)
        dirs.append(w)
        beta = beta_ref[h : h + 1, :]
        column = jnp.sum(jnp.where(row == col, beta, 0.0), axis=1, keepdims=True)
        lows.append(jnp.where(strict, dot(w, w, NT) * column, 0.0))
        betas.append(beta)
    corners = []
    for low in lows:
        corners += [low[:DH, :DH], low[DH:, DH:]]
    found = lower_inverses(corners, r, c)
    for h in range(2):
        first, second = found[2 * h], found[2 * h + 1]
        cross = -exact(second, exact(lows[h][DH:, :DH], first))
        upper = jnp.concatenate([first, jnp.zeros((DH, DH), F32)], axis=1)
        lower = jnp.concatenate([cross, second], axis=1)
        t = (jnp.concatenate([upper, lower], axis=0) * betas[h]).astype(BF16)
        w_ref[h] = dirs[h]
        t_ref[h] = t


def pieces_kernel(x_ref, out_ref, sems):
    copies = [pltpu.make_async_copy(x_ref, out_ref.at[p], sems.at[p]) for p in range(4)]
    for copy in copies:
        copy.start()
    for copy in copies:
        copy.wait()


def project_kernel(
    at_ref, hop_ref, x_ref, o_ref, wq_ref, wk_ref, wv_ref, w_ref, t_ref,
    mark_ref, p0_ref, p1_ref, q_ref, k_ref, v_ref, c_ref,
):
    def product(weights):
        total = None
        for p in range(4):
            for ref, c in ((x_ref, at_ref[1]), (o_ref, 1 - at_ref[1])):
                rows = pl.ds(pl.multiple_of((2 * p + c) * 256, 256), 256)
                term = dot(ref[p], weights[rows, :])
                total = term if total is None else total + term
        return total.astype(BF16)

    del mark_ref
    query, key, value = product(wq_ref), product(wk_ref), product(wv_ref)
    for h in range(2):
        cut = slice(h * DH, (h + 1) * DH)
        q_ref[h] = query[:, cut]
        k_ref[h] = key[:, cut]
        v_ref[h] = value[:, cut]
    row = lax.broadcasted_iota(jnp.int32, (TOK, TOK), 0)
    col = lax.broadcasted_iota(jnp.int32, (TOK, TOK), 1)
    hops = hop_ref[0].astype(F32)
    eye = (row == col).astype(F32)[:DH, :DH]
    for j, p_ref in enumerate((p0_ref, p1_ref)):
        h = lax.rem(at_ref[0] + j, 2)
        q, k, w, t = q_ref[h], k_ref[h], w_ref[h], t_ref[h]
        u = dot(t, w, TN).astype(BF16)
        qdirs = jnp.where(row >= col, dot(q, w, NT), 0.0).astype(BF16)
        keydirs = jnp.where(col > row, dot(k, w, NT), 0.0).astype(BF16)
        coef = dot(qdirs, t).astype(BF16)
        c_ref[h] = coef
        qhat = q.astype(F32) - dot(coef, w)
        p_ref[0:TOK] = (qhat * SCALE).astype(BF16)
        p_ref[TOK : 2 * TOK] = (k.astype(F32) - dot(keydirs, u)).astype(BF16)
        p_ref[2 * TOK : 3 * TOK] = v_ref[h]
        p_ref[3 * TOK : HOP_ROW] = (eye - dot(u, w, TN)).astype(BF16)
        p_ref[HOP_ROW:PACK] = jnp.full((16, DH), hops, F32).astype(BF16)


def own_kernel(q_ref, k_ref, v_ref, w_ref, c_ref, acc_ref, lse_ref):
    row = lax.broadcasted_iota(jnp.int32, (TOK, TOK), 0)
    col = lax.broadcasted_iota(jnp.int32, (TOK, TOK), 1)
    for h in range(2):
        q, k, w = q_ref[h], k_ref[h], w_ref[h]
        dirkeys = jnp.where(row > col, dot(w, k, NT), 0.0).astype(BF16)
        own = (dot(q, k, NT) - dot(c_ref[h], dirkeys)) * SCALE
        own = jnp.where(row >= col, own, NEG)
        top = jnp.max(own, axis=1, keepdims=True)
        prob = jnp.exp2(own - top)
        total = jnp.sum(prob, axis=1, keepdims=True)
        acc_ref[h] = dot(prob.astype(BF16), v_ref[h]) / total
        lse_ref[h] = jnp.broadcast_to(top + jnp.log2(total), (TOK, DH))


def pair_kernel(at_ref, r0_ref, r1_ref, q_ref, pair_ref, hop_ref):
    swapped = at_ref[0] == 1

    def part(low, high):
        a, b = r0_ref[low:high], r1_ref[low:high]
        return jnp.where(swapped, b, a), jnp.where(swapped, a, b)

    q_even, q_odd = part(0, TOK)
    k_even, k_odd = part(TOK, 2 * TOK)
    v_even, v_odd = part(2 * TOK, 3 * TOK)
    a_even, a_odd = part(3 * TOK, HOP_ROW)
    h_even, h_odd = part(HOP_ROW, PACK)
    pair_ref[0:TOK] = dot(k_even, a_odd, NT).astype(BF16)
    pair_ref[TOK : 2 * TOK] = k_odd
    pair_ref[2 * TOK : 3 * TOK] = v_even
    pair_ref[3 * TOK : 4 * TOK] = v_odd
    pair_ref[4 * TOK : PAIR] = dot(a_odd, a_even).astype(BF16)
    q_ref[0, 0] = q_even
    q_ref[0, 1] = q_odd
    q_ref[1, 0] = q_even
    q_ref[1, 1] = dot(q_odd, a_even).astype(BF16)
    q_ref[2, 0] = k_even
    q_ref[2, 1] = v_even
    hop_ref[0] = h_even.astype(F32)
    hop_ref[1] = h_odd.astype(F32)


def window_step(q, keys, d, i, hops, pair):
    col = lax.broadcasted_iota(jnp.int32, (1, 2 * TOK), 1)
    distance = 2 * d + i - (col >= TOK).astype(jnp.int32)
    valid = (distance.astype(F32) <= hops) & (pair >= d)
    return dot(q, keys[0 : 2 * TOK], NT) + jnp.where(valid, 0.0, NEG)


def near_kernel(at_ref, q_ref, hop_ref, d1_ref, d2_ref, acc_ref, top_ref, total_ref, next_ref):
    pair = at_ref[2]
    for i in range(2):
        hops = hop_ref[i, 0:1, 0:1]
        q = q_ref[1, i]
        first = window_step(q, d1_ref, 1, i, hops, pair)
        q = dot(q, d1_ref[4 * TOK : PAIR]).astype(BF16)
        second = window_step(q, d2_ref, 2, i, hops, pair)
        next_ref[i] = dot(q, d2_ref[4 * TOK : PAIR]).astype(BF16)
        top = jnp.maximum(jnp.max(first, axis=1, keepdims=True), jnp.max(second, axis=1, keepdims=True))
        if i == 1:
            inside = dot(q_ref[0, 1], q_ref[2, 0], NT)
            top = jnp.maximum(top, jnp.max(inside, axis=1, keepdims=True))
        first, second = jnp.exp2(first - top), jnp.exp2(second - top)
        total = jnp.sum(first, axis=1, keepdims=True) + jnp.sum(second, axis=1, keepdims=True)
        acc = dot(first.astype(BF16), d1_ref[2 * TOK : 4 * TOK])
        acc += dot(second.astype(BF16), d2_ref[2 * TOK : 4 * TOK])
        if i == 1:
            inside = jnp.exp2(inside - top)
            total += jnp.sum(inside, axis=1, keepdims=True)
            acc += dot(inside.astype(BF16), q_ref[2, 1])
        acc_ref[i] = acc
        top_ref[i] = jnp.broadcast_to(top, (TOK, DH))
        total_ref[i] = jnp.broadcast_to(total, (TOK, DH))


def far_kernel(
    at_ref, hop_ref, d3_ref, d4_ref, acc_ref, top_ref, total_ref, next_ref, o0_ref, o1_ref
):
    pair = at_ref[2]
    for j, out_ref in enumerate((o0_ref, o1_ref)):
        i = lax.rem(at_ref[0] + j, 2)
        hops = hop_ref[i, 0:1, 0:1]
        q = next_ref[i]
        third = window_step(q, d3_ref, 3, i, hops, pair)
        q = dot(q, d3_ref[4 * TOK : PAIR]).astype(BF16)
        fourth = window_step(q, d4_ref, 4, i, hops, pair)
        before = top_ref[i, :, 0:1]
        top = jnp.maximum(jnp.max(third, axis=1, keepdims=True), jnp.max(fourth, axis=1, keepdims=True))
        top = jnp.maximum(top, before)
        third, fourth = jnp.exp2(third - top), jnp.exp2(fourth - top)
        kept = jnp.exp2(before - top)
        total = total_ref[i, :, 0:1] * kept
        total += jnp.sum(third, axis=1, keepdims=True) + jnp.sum(fourth, axis=1, keepdims=True)
        acc = acc_ref[i] * kept
        acc += dot(third.astype(BF16), d3_ref[2 * TOK : 4 * TOK])
        acc += dot(fourth.astype(BF16), d4_ref[2 * TOK : 4 * TOK])
        out_ref[0:TOK] = (acc / total).astype(BF16)
        lse = jnp.broadcast_to(top + jnp.log2(total), (TOK, DH)).T[0:16]
        high = lse.astype(BF16).astype(F32)
        low = lse - high
        line = lax.broadcasted_iota(jnp.int32, (16, DH), 0)
        tile = jnp.where(line == 0, high[:, :DH], high[:, DH:])
        tile = jnp.where(line == 2, low[:, :DH], tile)
        tile = jnp.where(line == 3, low[:, DH:], tile)
        out_ref[TOK:BACK] = tile.astype(BF16)


def merge_kernel(at_ref, g0_ref, g1_ref, acc_ref, lse_ref, out_ref):
    swapped = at_ref[0] == 1
    row = lax.broadcasted_iota(jnp.int32, (DH, DH), 0)
    col = lax.broadcasted_iota(jnp.int32, (DH, DH), 1)
    for h in range(2):
        a, b = (g0_ref, g1_ref) if h == 0 else (g1_ref, g0_ref)
        got = jnp.where(swapped, b[...], a[...]).astype(F32)
        tile = got[TOK:BACK]
        column = []
        for part in range(2):
            line = tile[part : part + 1] + tile[part + 2 : part + 3]
            column.append(jnp.sum(jnp.where(row == col, line, 0.0), axis=1, keepdims=True))
        far = jnp.concatenate(column, axis=0)
        own = lse_ref[h, :, 0:1]
        top = jnp.maximum(own, far)
        mine, theirs = jnp.exp2(own - top), jnp.exp2(far - top)
        mixed = (acc_ref[h] * mine + got[:TOK] * theirs) / (mine + theirs)
        out_ref[:, h * DH : (h + 1) * DH] = mixed.astype(BF16)


def columns(c, p):
    return pl.ds(pl.multiple_of((2 * p + c) * 256, 256), 256)


def halves_kernel(at_ref, wo_ref, out_ref):
    for p in range(4):
        out_ref[p] = wo_ref[:, columns(1 - at_ref[1], p)]


def mine_kernel(at_ref, mine_ref, wo_ref, out_ref):
    for p in range(4):
        out_ref[p] = dot(mine_ref[...], wo_ref[:, columns(at_ref[1], p)])


def output_kernel(part_ref, theirs_ref, other_ref, out_ref):
    for p in range(4):
        out_ref[p] = (part_ref[p] + dot(theirs_ref[...], other_ref[p])).astype(BF16)


def sum_kernel(x_ref, out_ref):
    total = x_ref[0].astype(F32)
    for p in range(1, 4):
        total += x_ref[p].astype(F32)
    out_ref[...] = total.astype(BF16)


def regroup_pairs(j, rows, cross, groups):
    pairs = []
    for z in range(rows):
        for x in range(4):
            for y in range(groups):
                for c in range(2):
                    i = (x + j) % 2
                    pairs.append(((z * 4 + x) * cross + y * 2 + c, (z * 4 + 2 * c + i) * cross + y * 2 + x // 2))
    return pairs


def follow_pairs(rows, cross):
    pairs = []
    for b in range(4 * rows):
        for y in range(0, cross, 2):
            pairs.append((b * cross + y, b * cross + y + 1))
            if b + 4 < 4 * rows:
                pairs.append((b * cross + y + 1, (b + 4) * cross + y))
    return pairs


def shape(dims, dtype=BF16):
    return jax.ShapeDtypeStruct(dims, dtype)


def shards(inputs, w_query, w_key, w_value, w_out, reflect_dir, strength, hop_count):
    both = ("ctx", "head")
    z = lax.axis_index("ctx") // 4
    x = lax.axis_index("ctx") % 4
    c = lax.axis_index("head") % 2
    at = jnp.stack([x % 2, c, 2 * z + c]).astype(jnp.int32)
    there = [regroup_pairs(j, 16, 8, 4) for j in range(2)]
    back = [[(b, a) for a, b in pairs] for pairs in there]
    follow = follow_pairs(16, 8)
    down = [(b, b + 4) for b in range(60)]
    twin = [(h, h ^ 1) for h in range(8)]

    w, t, mark = call(
        directions_kernel, [shape((2, TOK, DH)), shape((2, TOK, TOK)), shape((8, DH), F32)], 2, flops=2**32
    )(reflect_dir, strength)
    planes = [[0, 2, 4, 6], [1, 3, 5, 7]]
    copies = pl.pallas_call(
        pieces_kernel,
        out_shape=shape((4, TOK, 256)),
        in_specs=[VMEM],
        out_specs=pl.BlockSpec(memory_space=pltpu.HBM),
        scratch_shapes=[pltpu.SemaphoreType.DMA((4,))],
        compiler_params=pltpu.CompilerParams(vmem_limit_bytes=62 * 2**20),
        cost_estimate=pl.CostEstimate(flops=0, bytes_accessed=2**20, transcendentals=0),
    )(inputs)
    gathered = lax.all_to_all(copies, "head", 0, 0, axis_index_groups=planes)
    gathered, mark = lax.optimization_barrier((gathered, mark))
    other = lax.ppermute(gathered, "head", twin)
    halves = call(halves_kernel, shape((4, 256, 256)), 2, smem=1)(at, w_out)
    other_out = lax.ppermute(halves, "head", twin)
    p0, p1, q, k, v, coef = call(
        project_kernel,
        [shape((PACK, DH)), shape((PACK, DH))] + [shape((2, TOK, DH))] * 3 + [shape((2, TOK, TOK))],
        9, smem=2, flops=2**30, late=1,
    )(at, hop_count, gathered, other, w_query, w_key, w_value, w, t, mark)
    r0 = lax.ppermute(p0, both, there[0])
    r1 = lax.ppermute(p1, both, there[1])
    acc, lse = call(
        own_kernel, [shape((2, TOK, DH), F32), shape((2, TOK, DH), F32)], 5, flops=2**31
    )(q, k, v, w, coef)
    qs, own_pair, hops = call(
        pair_kernel,
        [shape((3, 2, TOK, DH)), shape((PAIR, DH)), shape((2, 16, DH), F32)],
        3, smem=1, flops=2**28,
    )(at, r0, r1)
    d1 = lax.ppermute(own_pair, both, follow)
    d2 = lax.ppermute(own_pair, "ctx", down)
    d3 = lax.ppermute(d2, both, follow)
    d4 = lax.ppermute(d2, "ctx", down)
    state = [shape((2, TOK, DH), F32)] * 3 + [shape((2, TOK, DH))]
    near = call(near_kernel, state, 5, smem=1, flops=2**31)(at, qs, hops, d1, d2)
    o0, o1 = call(
        far_kernel, [shape((BACK, DH)), shape((BACK, DH))], 8, smem=1, flops=2**30
    )(at, hops, d3, d4, *near)
    g0 = lax.ppermute(o0, both, back[0])
    g1 = lax.ppermute(o1, both, back[1])
    mine = call(merge_kernel, shape((TOK, 2 * DH)), 5, smem=1, flops=2**28)(at, g0, g1, acc, lse)
    theirs = lax.ppermute(mine, "head", twin)
    part = call(mine_kernel, shape((4, TOK, 256), F32), 3, smem=1, flops=2**29)(at, mine, w_out)
    partial = call(output_kernel, shape((4, TOK, 256)), 3, flops=2**28)(part, theirs, other_out)
    pieces = lax.all_to_all(partial, "head", 0, 0, axis_index_groups=planes)
    return call(sum_kernel, shape((TOK, 256)), 1)(pieces)


def solution(mesh):
    placed = (
        P("ctx", "head"),
        P(None, "head"),
        P(None, "head"),
        P(None, "head"),
        P("head", None),
        P("ctx", "head"),
        P("head", "ctx"),
        P("ctx"),
    )
    return jax.shard_map(
        shards, mesh=mesh, in_specs=placed, out_specs=P("ctx", "head"), check_vma=False
    )
```

```python
import jax
import jax.numpy as jnp
from jax import lax
from jax.experimental import pallas as pl
from jax.experimental.pallas import tpu as pltpu
from jax.sharding import PartitionSpec as P

TOK = 256
DH = 128
SCALE = 1.4426950408889634 / DH**0.5
NEG = -1e30
F32 = jnp.float32
BF16 = jnp.bfloat16
HOP_ROW = 3 * TOK + DH
PACK = HOP_ROW + 16
PAIR = 4 * TOK + DH
BACK = TOK + 16
VMEM = pl.BlockSpec(memory_space=pltpu.VMEM)
SMEM = pl.BlockSpec(memory_space=pltpu.SMEM)

NN = (((1,), (0,)), ((), ()))
NT = (((1,), (1,)), ((), ()))
TN = (((0,), (0,)), ((), ()))


def dot(a, b, dims=NN):
    return lax.dot_general(a, b, dims, preferred_element_type=F32)


def split(a):
    high = a.astype(BF16)
    return high, (a - high.astype(F32)).astype(BF16)


def exact(a, b):
    (ah, al), (bh, bl) = split(a), split(b)
    return dot(ah, bh) + (dot(ah, bl) + dot(al, bh))


def call(body, outs, ins, flops=0, smem=0, late=0, scratch=()):
    return pl.pallas_call(
        body,
        out_shape=outs,
        in_specs=[SMEM] * smem + [VMEM] * (ins - smem) + [pl.BlockSpec(memory_space=pl.ANY)] * late,
        out_specs=jax.tree.map(lambda _: VMEM, outs),
        scratch_shapes=list(scratch),
        compiler_params=pltpu.CompilerParams(vmem_limit_bytes=48 * 2**20),
        cost_estimate=pl.CostEstimate(flops=flops, bytes_accessed=2**20, transcendentals=0),
    )


def lower_inverses(blocks, row, col):
    eye = (row == col).astype(F32)
    same = (row // 4) == (col // 4)
    small = [jnp.where(same, b, 0.0) for b in blocks]
    squares = [exact(s, s) for s in small]
    found = [exact(eye - s, eye + q) for s, q in zip(small, squares)]
    size = 4
    while size < DH:
        off = ((row // (2 * size)) == (col // (2 * size))) & ((row // size) != (col // size))
        left = [exact(x, jnp.where(off, b, 0.0)) for x, b in zip(found, blocks)]
        found = [x - exact(y, x) for x, y in zip(found, left)]
        size *= 2
    return found


def directions_kernel(dirs_ref, beta_ref, w_ref, t_ref, mark_ref):
    mark_ref[...] = jnp.zeros((8, DH), F32)
    row = lax.broadcasted_iota(jnp.int32, (TOK, TOK), 0)
    col = lax.broadcasted_iota(jnp.int32, (TOK, TOK), 1)
    strict = row > col
    r, c = row[:DH, :DH], col[:DH, :DH]
    dirs, lows, betas = [], [], []
    for h in range(2):
        d = dirs_ref[:, h * DH : (h + 1) * DH].astype(F32)
        d = d * lax.rsqrt(jnp.sum(d * d, axis=1, keepdims=True) + 1e-6)
        w = d.astype(BF16)
        dirs.append(w)
        beta = beta_ref[h : h + 1, :]
        column = jnp.sum(jnp.where(row == col, beta, 0.0), axis=1, keepdims=True)
        lows.append(jnp.where(strict, dot(w, w, NT) * column, 0.0))
        betas.append(beta)
    corners = []
    for low in lows:
        corners += [low[:DH, :DH], low[DH:, DH:]]
    found = lower_inverses(corners, r, c)
    for h in range(2):
        first, second = found[2 * h], found[2 * h + 1]
        cross = -exact(second, exact(lows[h][DH:, :DH], first))
        upper = jnp.concatenate([first, jnp.zeros((DH, DH), F32)], axis=1)
        lower = jnp.concatenate([cross, second], axis=1)
        t = (jnp.concatenate([upper, lower], axis=0) * betas[h]).astype(BF16)
        w_ref[h] = dirs[h]
        t_ref[h] = t


def pieces_kernel(x_ref, out_ref, sems):
    copies = [pltpu.make_async_copy(x_ref, out_ref.at[p], sems.at[p]) for p in range(4)]
    for copy in copies:
        copy.start()
    for copy in copies:
        copy.wait()


def project_kernel(
    at_ref, hop_ref, x_ref, o_ref, wq_ref, wk_ref, wv_ref, w_ref, t_ref,
    mark_ref, p0_ref, p1_ref, q_ref, k_ref, v_ref, c_ref,
):
    def product(weights):
        total = None
        for p in range(4):
            for ref, c in ((x_ref, at_ref[1]), (o_ref, 1 - at_ref[1])):
                rows = pl.ds(pl.multiple_of((2 * p + c) * 256, 256), 256)
                term = dot(ref[p], weights[rows, :])
                total = term if total is None else total + term
        return total.astype(BF16)

    del mark_ref
    query, key, value = product(wq_ref), product(wk_ref), product(wv_ref)
    for h in range(2):
        cut = slice(h * DH, (h + 1) * DH)
        q_ref[h] = query[:, cut]
        k_ref[h] = key[:, cut]
        v_ref[h] = value[:, cut]
    row = lax.broadcasted_iota(jnp.int32, (TOK, TOK), 0)
    col = lax.broadcasted_iota(jnp.int32, (TOK, TOK), 1)
    hops = hop_ref[0].astype(F32)
    eye = (row == col).astype(F32)[:DH, :DH]
    for j, p_ref in enumerate((p0_ref, p1_ref)):
        h = lax.rem(at_ref[0] + j, 2)
        q, k, w, t = q_ref[h], k_ref[h], w_ref[h], t_ref[h]
        u = dot(t, w, TN).astype(BF16)
        qdirs = jnp.where(row >= col, dot(q, w, NT), 0.0).astype(BF16)
        keydirs = jnp.where(col > row, dot(k, w, NT), 0.0).astype(BF16)
        coef = dot(qdirs, t).astype(BF16)
        c_ref[h] = coef
        qhat = q.astype(F32) - dot(coef, w)
        p_ref[0:TOK] = (qhat * SCALE).astype(BF16)
        p_ref[TOK : 2 * TOK] = (k.astype(F32) - dot(keydirs, u)).astype(BF16)
        p_ref[2 * TOK : 3 * TOK] = v_ref[h]
        p_ref[3 * TOK : HOP_ROW] = (eye - dot(u, w, TN)).astype(BF16)
        p_ref[HOP_ROW:PACK] = jnp.full((16, DH), hops, F32).astype(BF16)


def own_kernel(q_ref, k_ref, v_ref, w_ref, c_ref, acc_ref, lse_ref):
    row = lax.broadcasted_iota(jnp.int32, (TOK, TOK), 0)
    col = lax.broadcasted_iota(jnp.int32, (TOK, TOK), 1)
    for h in range(2):
        q, k, w = q_ref[h], k_ref[h], w_ref[h]
        dirkeys = jnp.where(row > col, dot(w, k, NT), 0.0).astype(BF16)
        own = (dot(q, k, NT) - dot(c_ref[h], dirkeys)) * SCALE
        own = jnp.where(row >= col, own, NEG)
        top = jnp.max(own, axis=1, keepdims=True)
        prob = jnp.exp2(own - top)
        total = jnp.sum(prob, axis=1, keepdims=True)
        acc_ref[h] = dot(prob.astype(BF16), v_ref[h]) / total
        lse_ref[h] = jnp.broadcast_to(top + jnp.log2(total), (TOK, DH))


def pair_kernel(at_ref, r0_ref, r1_ref, q_ref, pair_ref, hop_ref):
    swapped = at_ref[0] == 1

    def part(low, high):
        a, b = r0_ref[low:high], r1_ref[low:high]
        return jnp.where(swapped, b, a), jnp.where(swapped, a, b)

    q_even, q_odd = part(0, TOK)
    k_even, k_odd = part(TOK, 2 * TOK)
    v_even, v_odd = part(2 * TOK, 3 * TOK)
    a_even, a_odd = part(3 * TOK, HOP_ROW)
    h_even, h_odd = part(HOP_ROW, PACK)
    pair_ref[0:TOK] = dot(k_even, a_odd, NT).astype(BF16)
    pair_ref[TOK : 2 * TOK] = k_odd
    pair_ref[2 * TOK : 3 * TOK] = v_even
    pair_ref[3 * TOK : 4 * TOK] = v_odd
    pair_ref[4 * TOK : PAIR] = dot(a_odd, a_even).astype(BF16)
    q_ref[0, 0] = q_even
    q_ref[0, 1] = q_odd
    q_ref[1, 0] = q_even
    q_ref[1, 1] = dot(q_odd, a_even).astype(BF16)
    q_ref[2, 0] = k_even
    q_ref[2, 1] = v_even
    hop_ref[0] = h_even.astype(F32)
    hop_ref[1] = h_odd.astype(F32)


def window_step(q, keys, d, i, hops, pair):
    col = lax.broadcasted_iota(jnp.int32, (1, 2 * TOK), 1)
    distance = 2 * d + i - (col >= TOK).astype(jnp.int32)
    valid = (distance.astype(F32) <= hops) & (pair >= d)
    return dot(q, keys[0 : 2 * TOK], NT) + jnp.where(valid, 0.0, NEG)


def near_kernel(at_ref, q_ref, hop_ref, d1_ref, d2_ref, acc_ref, top_ref, total_ref, next_ref):
    pair = at_ref[2]
    for i in range(2):
        hops = hop_ref[i, 0:1, 0:1]
        q = q_ref[1, i]
        first = window_step(q, d1_ref, 1, i, hops, pair)
        q = dot(q, d1_ref[4 * TOK : PAIR]).astype(BF16)
        second = window_step(q, d2_ref, 2, i, hops, pair)
        next_ref[i] = dot(q, d2_ref[4 * TOK : PAIR]).astype(BF16)
        top = jnp.maximum(jnp.max(first, axis=1, keepdims=True), jnp.max(second, axis=1, keepdims=True))
        if i == 1:
            inside = dot(q_ref[0, 1], q_ref[2, 0], NT)
            top = jnp.maximum(top, jnp.max(inside, axis=1, keepdims=True))
        first, second = jnp.exp2(first - top), jnp.exp2(second - top)
        total = jnp.sum(first, axis=1, keepdims=True) + jnp.sum(second, axis=1, keepdims=True)
        acc = dot(first.astype(BF16), d1_ref[2 * TOK : 4 * TOK])
        acc += dot(second.astype(BF16), d2_ref[2 * TOK : 4 * TOK])
        if i == 1:
            inside = jnp.exp2(inside - top)
            total += jnp.sum(inside, axis=1, keepdims=True)
            acc += dot(inside.astype(BF16), q_ref[2, 1])
        acc_ref[i] = acc
        top_ref[i] = jnp.broadcast_to(top, (TOK, DH))
        total_ref[i] = jnp.broadcast_to(total, (TOK, DH))


def grown(q, keys, d, i, hops, pair, acc_ref, top_ref, total_ref):
    scores = window_step(q, keys, d, i, hops, pair)
    before = top_ref[i, :, 0:1]
    top = jnp.maximum(jnp.max(scores, axis=1, keepdims=True), before)
    prob = jnp.exp2(scores - top)
    kept = jnp.exp2(before - top)
    total = total_ref[i, :, 0:1] * kept + jnp.sum(prob, axis=1, keepdims=True)
    acc = acc_ref[i] * kept + dot(prob.astype(BF16), keys[2 * TOK : 4 * TOK])
    return acc, top, total


def middle_kernel(
    at_ref, hop_ref, d3_ref, acc_ref, top_ref, total_ref, q_ref, acc_out, top_out, total_out, next_ref
):
    for i in range(2):
        q, hops = q_ref[i], hop_ref[i, 0:1, 0:1]
        acc, top, total = grown(q, d3_ref, 3, i, hops, at_ref[2], acc_ref, top_ref, total_ref)
        acc_out[i] = acc
        top_out[i] = jnp.broadcast_to(top, (TOK, DH))
        total_out[i] = jnp.broadcast_to(total, (TOK, DH))
        next_ref[i] = dot(q, d3_ref[4 * TOK : PAIR]).astype(BF16)


def far_kernel(at_ref, hop_ref, d4_ref, acc_ref, top_ref, total_ref, q_ref, o0_ref, o1_ref):
    for j, out_ref in enumerate((o0_ref, o1_ref)):
        i = lax.rem(at_ref[0] + j, 2)
        hops = hop_ref[i, 0:1, 0:1]
        acc, top, total = grown(q_ref[i], d4_ref, 4, i, hops, at_ref[2], acc_ref, top_ref, total_ref)
        out_ref[0:TOK] = (acc / total).astype(BF16)
        lse = jnp.broadcast_to(top + jnp.log2(total), (TOK, DH)).T[0:16]
        high = lse.astype(BF16).astype(F32)
        low = lse - high
        line = lax.broadcasted_iota(jnp.int32, (16, DH), 0)
        tile = jnp.where(line == 0, high[:, :DH], high[:, DH:])
        tile = jnp.where(line == 2, low[:, :DH], tile)
        tile = jnp.where(line == 3, low[:, DH:], tile)
        out_ref[TOK:BACK] = tile.astype(BF16)


def merge_kernel(at_ref, g0_ref, g1_ref, acc_ref, lse_ref, out_ref):
    swapped = at_ref[0] == 1
    row = lax.broadcasted_iota(jnp.int32, (DH, DH), 0)
    col = lax.broadcasted_iota(jnp.int32, (DH, DH), 1)
    for h in range(2):
        a, b = (g0_ref, g1_ref) if h == 0 else (g1_ref, g0_ref)
        got = jnp.where(swapped, b[...], a[...]).astype(F32)
        tile = got[TOK:BACK]
        column = []
        for part in range(2):
            line = tile[part : part + 1] + tile[part + 2 : part + 3]
            column.append(jnp.sum(jnp.where(row == col, line, 0.0), axis=1, keepdims=True))
        far = jnp.concatenate(column, axis=0)
        own = lse_ref[h, :, 0:1]
        top = jnp.maximum(own, far)
        mine, theirs = jnp.exp2(own - top), jnp.exp2(far - top)
        mixed = (acc_ref[h] * mine + got[:TOK] * theirs) / (mine + theirs)
        out_ref[:, h * DH : (h + 1) * DH] = mixed.astype(BF16)


def columns(c, p):
    return pl.ds(pl.multiple_of((2 * p + c) * 256, 256), 256)


def halves_kernel(at_ref, wo_ref, out_ref):
    for p in range(4):
        out_ref[p] = wo_ref[:, columns(1 - at_ref[1], p)]


def mine_kernel(at_ref, mine_ref, wo_ref, out_ref):
    for p in range(4):
        out_ref[p] = dot(mine_ref[...], wo_ref[:, columns(at_ref[1], p)])


def output_kernel(part_ref, theirs_ref, other_ref, out_ref):
    for p in range(4):
        out_ref[p] = (part_ref[p] + dot(theirs_ref[...], other_ref[p])).astype(BF16)


def sum_kernel(x_ref, out_ref):
    total = x_ref[0].astype(F32)
    for p in range(1, 4):
        total += x_ref[p].astype(F32)
    out_ref[...] = total.astype(BF16)


def regroup_pairs(j, rows, cross, groups):
    pairs = []
    for z in range(rows):
        for x in range(4):
            for y in range(groups):
                for c in range(2):
                    i = (x + j) % 2
                    pairs.append(((z * 4 + x) * cross + y * 2 + c, (z * 4 + 2 * c + i) * cross + y * 2 + x // 2))
    return pairs


def follow_pairs(rows, cross):
    pairs = []
    for b in range(4 * rows):
        for y in range(0, cross, 2):
            pairs.append((b * cross + y, b * cross + y + 1))
            if b + 4 < 4 * rows:
                pairs.append((b * cross + y + 1, (b + 4) * cross + y))
    return pairs


def shape(dims, dtype=BF16):
    return jax.ShapeDtypeStruct(dims, dtype)


def shards(inputs, w_query, w_key, w_value, w_out, reflect_dir, strength, hop_count):
    both = ("ctx", "head")
    z = lax.axis_index("ctx") // 4
    x = lax.axis_index("ctx") % 4
    c = lax.axis_index("head") % 2
    at = jnp.stack([x % 2, c, 2 * z + c]).astype(jnp.int32)
    there = [regroup_pairs(j, 16, 8, 4) for j in range(2)]
    back = [[(b, a) for a, b in pairs] for pairs in there]
    follow = follow_pairs(16, 8)
    down = [(b, b + 4) for b in range(60)]
    twin = [(h, h ^ 1) for h in range(8)]

    w, t, mark = call(
        directions_kernel, [shape((2, TOK, DH)), shape((2, TOK, TOK)), shape((8, DH), F32)], 2, flops=2**32
    )(reflect_dir, strength)
    planes = [[0, 2, 4, 6], [1, 3, 5, 7]]
    copies = pl.pallas_call(
        pieces_kernel,
        out_shape=shape((4, TOK, 256)),
        in_specs=[VMEM],
        out_specs=pl.BlockSpec(memory_space=pltpu.HBM),
        scratch_shapes=[pltpu.SemaphoreType.DMA((4,))],
        compiler_params=pltpu.CompilerParams(vmem_limit_bytes=62 * 2**20),
        cost_estimate=pl.CostEstimate(flops=0, bytes_accessed=2**20, transcendentals=0),
    )(inputs)
    gathered = lax.all_to_all(copies, "head", 0, 0, axis_index_groups=planes)
    gathered, mark = lax.optimization_barrier((gathered, mark))
    other = lax.ppermute(gathered, "head", twin)
    halves = call(halves_kernel, shape((4, 256, 256)), 2, smem=1)(at, w_out)
    other_out = lax.ppermute(halves, "head", twin)
    p0, p1, q, k, v, coef = call(
        project_kernel,
        [shape((PACK, DH)), shape((PACK, DH))] + [shape((2, TOK, DH))] * 3 + [shape((2, TOK, TOK))],
        9, smem=2, flops=2**30, late=1,
    )(at, hop_count, gathered, other, w_query, w_key, w_value, w, t, mark)
    r0 = lax.ppermute(p0, both, there[0])
    r1 = lax.ppermute(p1, both, there[1])
    acc, lse = call(
        own_kernel, [shape((2, TOK, DH), F32), shape((2, TOK, DH), F32)], 5, flops=2**31
    )(q, k, v, w, coef)
    qs, own_pair, hops = call(
        pair_kernel,
        [shape((3, 2, TOK, DH)), shape((PAIR, DH)), shape((2, 16, DH), F32)],
        3, smem=1, flops=2**28,
    )(at, r0, r1)
    d1 = lax.ppermute(own_pair, both, follow)
    d2 = lax.ppermute(own_pair, "ctx", down)
    d2, other_out = lax.optimization_barrier((d2, other_out))
    d3 = lax.ppermute(d2, both, follow)
    d4 = lax.ppermute(d2, "ctx", down)
    state = [shape((2, TOK, DH), F32)] * 3 + [shape((2, TOK, DH))]
    near = call(near_kernel, state, 5, smem=1, flops=2**31)(at, qs, hops, d1, d2)
    middle = call(middle_kernel, state, 7, smem=1, flops=2**30)(at, hops, d3, *near)
    o0, o1 = call(far_kernel, [shape((BACK, DH)), shape((BACK, DH))], 7, smem=1, flops=2**30)(
        at, hops, d4, *middle
    )
    g0 = lax.ppermute(o0, both, back[0])
    g1 = lax.ppermute(o1, both, back[1])
    mine = call(merge_kernel, shape((TOK, 2 * DH)), 5, smem=1, flops=2**28)(at, g0, g1, acc, lse)
    theirs = lax.ppermute(mine, "head", twin)
    part = call(mine_kernel, shape((4, TOK, 256), F32), 3, smem=1, flops=2**29)(at, mine, w_out)
    partial = call(output_kernel, shape((4, TOK, 256)), 3, flops=2**28)(part, theirs, other_out)
    pieces = lax.all_to_all(partial, "head", 0, 0, axis_index_groups=planes)
    return call(sum_kernel, shape((TOK, 256)), 1)(pieces)


def solution(mesh):
    placed = (
        P("ctx", "head"),
        P(None, "head"),
        P(None, "head"),
        P(None, "head"),
        P("head", None),
        P("ctx", "head"),
        P("head", "ctx"),
        P("ctx"),
    )
    return jax.shard_map(
        shards, mesh=mesh, in_specs=placed, out_specs=P("ctx", "head"), check_vma=False
    )
```

```python
import jax
import jax.numpy as jnp
from jax import lax
from jax.experimental import pallas as pl
from jax.experimental.pallas import tpu as pltpu
from jax.sharding import PartitionSpec as P

TOK = 256
DH = 128
SCALE = 1.4426950408889634 / DH**0.5
NEG = -1e30
F32 = jnp.float32
BF16 = jnp.bfloat16
HOP_ROW = 3 * TOK + DH
PACK = HOP_ROW + 16
PAIR = 4 * TOK + DH
BACK = TOK + 16
VMEM = pl.BlockSpec(memory_space=pltpu.VMEM)
SMEM = pl.BlockSpec(memory_space=pltpu.SMEM)

NN = (((1,), (0,)), ((), ()))
NT = (((1,), (1,)), ((), ()))
TN = (((0,), (0,)), ((), ()))


def dot(a, b, dims=NN):
    return lax.dot_general(a, b, dims, preferred_element_type=F32)


def split(a):
    high = a.astype(BF16)
    return high, (a - high.astype(F32)).astype(BF16)


def exact(a, b):
    (ah, al), (bh, bl) = split(a), split(b)
    return dot(ah, bh) + (dot(ah, bl) + dot(al, bh))


def call(body, outs, ins, flops=0, smem=0, late=0, scratch=()):
    return pl.pallas_call(
        body,
        out_shape=outs,
        in_specs=[SMEM] * smem + [VMEM] * (ins - smem) + [pl.BlockSpec(memory_space=pl.ANY)] * late,
        out_specs=jax.tree.map(lambda _: VMEM, outs),
        scratch_shapes=list(scratch),
        compiler_params=pltpu.CompilerParams(vmem_limit_bytes=48 * 2**20),
        cost_estimate=pl.CostEstimate(flops=flops, bytes_accessed=2**20, transcendentals=0),
    )


def lower_inverses(blocks, row, col):
    eye = (row == col).astype(F32)
    same = (row // 4) == (col // 4)
    small = [jnp.where(same, b, 0.0) for b in blocks]
    squares = [exact(s, s) for s in small]
    found = [exact(eye - s, eye + q) for s, q in zip(small, squares)]
    size = 4
    while size < DH:
        off = ((row // (2 * size)) == (col // (2 * size))) & ((row // size) != (col // size))
        left = [exact(x, jnp.where(off, b, 0.0)) for x, b in zip(found, blocks)]
        found = [x - exact(y, x) for x, y in zip(found, left)]
        size *= 2
    return found


def directions_kernel(dirs_ref, beta_ref, w_ref, t_ref, mark_ref):
    mark_ref[...] = jnp.zeros((8, DH), F32)
    row = lax.broadcasted_iota(jnp.int32, (TOK, TOK), 0)
    col = lax.broadcasted_iota(jnp.int32, (TOK, TOK), 1)
    strict = row > col
    r, c = row[:DH, :DH], col[:DH, :DH]
    dirs, lows, betas = [], [], []
    for h in range(2):
        d = dirs_ref[:, h * DH : (h + 1) * DH].astype(F32)
        d = d * lax.rsqrt(jnp.sum(d * d, axis=1, keepdims=True) + 1e-6)
        w = d.astype(BF16)
        dirs.append(w)
        beta = beta_ref[h : h + 1, :]
        column = jnp.sum(jnp.where(row == col, beta, 0.0), axis=1, keepdims=True)
        lows.append(jnp.where(strict, dot(w, w, NT) * column, 0.0))
        betas.append(beta)
    corners = []
    for low in lows:
        corners += [low[:DH, :DH], low[DH:, DH:]]
    found = lower_inverses(corners, r, c)
    for h in range(2):
        first, second = found[2 * h], found[2 * h + 1]
        cross = -exact(second, exact(lows[h][DH:, :DH], first))
        upper = jnp.concatenate([first, jnp.zeros((DH, DH), F32)], axis=1)
        lower = jnp.concatenate([cross, second], axis=1)
        t = (jnp.concatenate([upper, lower], axis=0) * betas[h]).astype(BF16)
        w_ref[h] = dirs[h]
        t_ref[h] = t


def pieces_kernel(x_ref, out_ref, sems):
    copies = [pltpu.make_async_copy(x_ref, out_ref.at[p], sems.at[p]) for p in range(4)]
    for copy in copies:
        copy.start()
    for copy in copies:
        copy.wait()


def project_kernel(
    at_ref, hop_ref, x_ref, o_ref, wq_ref, wk_ref, wv_ref, w_ref, t_ref,
    mark_ref, p0_ref, p1_ref, q_ref, k_ref, v_ref, c_ref,
):
    def product(weights):
        total = None
        for p in range(4):
            for ref, c in ((x_ref, at_ref[1]), (o_ref, 1 - at_ref[1])):
                rows = pl.ds(pl.multiple_of((2 * p + c) * 256, 256), 256)
                term = dot(ref[p], weights[rows, :])
                total = term if total is None else total + term
        return total.astype(BF16)

    del mark_ref
    query, key, value = product(wq_ref), product(wk_ref), product(wv_ref)
    for h in range(2):
        cut = slice(h * DH, (h + 1) * DH)
        q_ref[h] = query[:, cut]
        k_ref[h] = key[:, cut]
        v_ref[h] = value[:, cut]
    row = lax.broadcasted_iota(jnp.int32, (TOK, TOK), 0)
    col = lax.broadcasted_iota(jnp.int32, (TOK, TOK), 1)
    hops = hop_ref[0].astype(F32)
    eye = (row == col).astype(F32)[:DH, :DH]
    for j, p_ref in enumerate((p0_ref, p1_ref)):
        h = lax.rem(at_ref[0] + j, 2)
        q, k, w, t = q_ref[h], k_ref[h], w_ref[h], t_ref[h]
        u = dot(t, w, TN).astype(BF16)
        qdirs = jnp.where(row >= col, dot(q, w, NT), 0.0).astype(BF16)
        keydirs = jnp.where(col > row, dot(k, w, NT), 0.0).astype(BF16)
        coef = dot(qdirs, t).astype(BF16)
        c_ref[h] = coef
        qhat = q.astype(F32) - dot(coef, w)
        p_ref[0:TOK] = (qhat * SCALE).astype(BF16)
        p_ref[TOK : 2 * TOK] = (k.astype(F32) - dot(keydirs, u)).astype(BF16)
        p_ref[2 * TOK : 3 * TOK] = v_ref[h]
        p_ref[3 * TOK : HOP_ROW] = (eye - dot(u, w, TN)).astype(BF16)
        p_ref[HOP_ROW:PACK] = jnp.full((16, DH), hops, F32).astype(BF16)


def own_kernel(q_ref, k_ref, v_ref, w_ref, c_ref, acc_ref, lse_ref):
    row = lax.broadcasted_iota(jnp.int32, (TOK, TOK), 0)
    col = lax.broadcasted_iota(jnp.int32, (TOK, TOK), 1)
    for h in range(2):
        q, k, w = q_ref[h], k_ref[h], w_ref[h]
        dirkeys = jnp.where(row > col, dot(w, k, NT), 0.0).astype(BF16)
        own = (dot(q, k, NT) - dot(c_ref[h], dirkeys)) * SCALE
        own = jnp.where(row >= col, own, NEG)
        top = jnp.max(own, axis=1, keepdims=True)
        prob = jnp.exp2(own - top)
        total = jnp.sum(prob, axis=1, keepdims=True)
        acc_ref[h] = dot(prob.astype(BF16), v_ref[h]) / total
        lse_ref[h] = jnp.broadcast_to(top + jnp.log2(total), (TOK, DH))


def pair_kernel(at_ref, r0_ref, r1_ref, q_ref, pair_ref, hop_ref):
    swapped = at_ref[0] == 1

    def part(low, high):
        a, b = r0_ref[low:high], r1_ref[low:high]
        return jnp.where(swapped, b, a), jnp.where(swapped, a, b)

    q_even, q_odd = part(0, TOK)
    k_even, k_odd = part(TOK, 2 * TOK)
    v_even, v_odd = part(2 * TOK, 3 * TOK)
    a_even, a_odd = part(3 * TOK, HOP_ROW)
    h_even, h_odd = part(HOP_ROW, PACK)
    pair_ref[0:TOK] = dot(k_even, a_odd, NT).astype(BF16)
    pair_ref[TOK : 2 * TOK] = k_odd
    pair_ref[2 * TOK : 3 * TOK] = v_even
    pair_ref[3 * TOK : 4 * TOK] = v_odd
    pair_ref[4 * TOK : PAIR] = dot(a_odd, a_even).astype(BF16)
    q_ref[0, 0] = q_even
    q_ref[0, 1] = q_odd
    q_ref[1, 0] = q_even
    q_ref[1, 1] = dot(q_odd, a_even).astype(BF16)
    q_ref[2, 0] = k_even
    q_ref[2, 1] = v_even
    hop_ref[0] = h_even.astype(F32)
    hop_ref[1] = h_odd.astype(F32)


def window_step(q, keys, d, i, hops, pair):
    col = lax.broadcasted_iota(jnp.int32, (1, 2 * TOK), 1)
    distance = 2 * d + i - (col >= TOK).astype(jnp.int32)
    valid = (distance.astype(F32) <= hops) & (pair >= d)
    return dot(q, keys[0 : 2 * TOK], NT) + jnp.where(valid, 0.0, NEG)


def near_kernel(at_ref, q_ref, hop_ref, d1_ref, d2_ref, acc_ref, top_ref, total_ref, next_ref):
    pair = at_ref[2]
    for i in range(2):
        hops = hop_ref[i, 0:1, 0:1]
        q = q_ref[1, i]
        first = window_step(q, d1_ref, 1, i, hops, pair)
        q = dot(q, d1_ref[4 * TOK : PAIR]).astype(BF16)
        second = window_step(q, d2_ref, 2, i, hops, pair)
        next_ref[i] = dot(q, d2_ref[4 * TOK : PAIR]).astype(BF16)
        top = jnp.maximum(jnp.max(first, axis=1, keepdims=True), jnp.max(second, axis=1, keepdims=True))
        if i == 1:
            inside = dot(q_ref[0, 1], q_ref[2, 0], NT)
            top = jnp.maximum(top, jnp.max(inside, axis=1, keepdims=True))
        first, second = jnp.exp2(first - top), jnp.exp2(second - top)
        total = jnp.sum(first, axis=1, keepdims=True) + jnp.sum(second, axis=1, keepdims=True)
        acc = dot(first.astype(BF16), d1_ref[2 * TOK : 4 * TOK])
        acc += dot(second.astype(BF16), d2_ref[2 * TOK : 4 * TOK])
        if i == 1:
            inside = jnp.exp2(inside - top)
            total += jnp.sum(inside, axis=1, keepdims=True)
            acc += dot(inside.astype(BF16), q_ref[2, 1])
        acc_ref[i] = acc
        top_ref[i] = jnp.broadcast_to(top, (TOK, DH))
        total_ref[i] = jnp.broadcast_to(total, (TOK, DH))


def grown(q, keys, d, i, hops, pair, acc_ref, top_ref, total_ref):
    scores = window_step(q, keys, d, i, hops, pair)
    before = top_ref[i, :, 0:1]
    top = jnp.maximum(jnp.max(scores, axis=1, keepdims=True), before)
    prob = jnp.exp2(scores - top)
    kept = jnp.exp2(before - top)
    total = total_ref[i, :, 0:1] * kept + jnp.sum(prob, axis=1, keepdims=True)
    acc = acc_ref[i] * kept + dot(prob.astype(BF16), keys[2 * TOK : 4 * TOK])
    return acc, top, total


def middle_kernel(
    at_ref, hop_ref, d3_ref, acc_ref, top_ref, total_ref, q_ref, acc_out, top_out, total_out, next_ref
):
    for i in range(2):
        q, hops = q_ref[i], hop_ref[i, 0:1, 0:1]
        acc, top, total = grown(q, d3_ref, 3, i, hops, at_ref[2], acc_ref, top_ref, total_ref)
        acc_out[i] = acc
        top_out[i] = jnp.broadcast_to(top, (TOK, DH))
        total_out[i] = jnp.broadcast_to(total, (TOK, DH))
        next_ref[i] = dot(q, d3_ref[4 * TOK : PAIR]).astype(BF16)


def far_kernel(at_ref, hop_ref, d4_ref, acc_ref, top_ref, total_ref, q_ref, o0_ref, o1_ref):
    for j, out_ref in enumerate((o0_ref, o1_ref)):
        i = lax.rem(at_ref[0] + j, 2)
        hops = hop_ref[i, 0:1, 0:1]
        acc, top, total = grown(q_ref[i], d4_ref, 4, i, hops, at_ref[2], acc_ref, top_ref, total_ref)
        out_ref[0:TOK] = (acc / total).astype(BF16)
        lse = jnp.broadcast_to(top + jnp.log2(total), (TOK, DH)).T[0:16]
        high = lse.astype(BF16).astype(F32)
        low = lse - high
        line = lax.broadcasted_iota(jnp.int32, (16, DH), 0)
        tile = jnp.where(line == 0, high[:, :DH], high[:, DH:])
        tile = jnp.where(line == 2, low[:, :DH], tile)
        tile = jnp.where(line == 3, low[:, DH:], tile)
        out_ref[TOK:BACK] = tile.astype(BF16)


def merge_kernel(at_ref, g1_ref, g0_ref, acc_ref, lse_ref, out_ref):
    swapped = at_ref[0] == 1
    row = lax.broadcasted_iota(jnp.int32, (DH, DH), 0)
    col = lax.broadcasted_iota(jnp.int32, (DH, DH), 1)
    for h in range(2):
        a, b = (g0_ref, g1_ref) if h == 0 else (g1_ref, g0_ref)
        got = jnp.where(swapped, b[...], a[...]).astype(F32)
        tile = got[TOK:BACK]
        column = []
        for part in range(2):
            line = tile[part : part + 1] + tile[part + 2 : part + 3]
            column.append(jnp.sum(jnp.where(row == col, line, 0.0), axis=1, keepdims=True))
        far = jnp.concatenate(column, axis=0)
        own = lse_ref[h, :, 0:1]
        top = jnp.maximum(own, far)
        mine, theirs = jnp.exp2(own - top), jnp.exp2(far - top)
        mixed = (acc_ref[h] * mine + got[:TOK] * theirs) / (mine + theirs)
        out_ref[:, h * DH : (h + 1) * DH] = mixed.astype(BF16)


def columns(c, p):
    return pl.ds(pl.multiple_of((2 * p + c) * 256, 256), 256)


def halves_kernel(at_ref, wo_ref, out_ref):
    for p in range(4):
        out_ref[p] = wo_ref[:, columns(1 - at_ref[1], p)]


def mine_kernel(at_ref, mine_ref, wo_ref, out_ref):
    for p in range(4):
        out_ref[p] = dot(mine_ref[...], wo_ref[:, columns(at_ref[1], p)])


def output_kernel(part_ref, theirs_ref, other_ref, out_ref):
    for p in range(4):
        out_ref[p] = (part_ref[p] + dot(theirs_ref[...], other_ref[p])).astype(BF16)


def sum_kernel(x_ref, out_ref):
    total = x_ref[0].astype(F32)
    for p in range(1, 4):
        total += x_ref[p].astype(F32)
    out_ref[...] = total.astype(BF16)


def regroup_pairs(j, rows, cross, groups):
    pairs = []
    for z in range(rows):
        for x in range(4):
            for y in range(groups):
                for c in range(2):
                    i = (x + j) % 2
                    pairs.append(((z * 4 + x) * cross + y * 2 + c, (z * 4 + 2 * c + i) * cross + y * 2 + x // 2))
    return pairs


def follow_pairs(rows, cross):
    pairs = []
    for b in range(4 * rows):
        for y in range(0, cross, 2):
            pairs.append((b * cross + y, b * cross + y + 1))
            if b + 4 < 4 * rows:
                pairs.append((b * cross + y + 1, (b + 4) * cross + y))
    return pairs


def shape(dims, dtype=BF16):
    return jax.ShapeDtypeStruct(dims, dtype)


def shards(inputs, w_query, w_key, w_value, w_out, reflect_dir, strength, hop_count):
    both = ("ctx", "head")
    z = lax.axis_index("ctx") // 4
    x = lax.axis_index("ctx") % 4
    c = lax.axis_index("head") % 2
    at = jnp.stack([x % 2, c, 2 * z + c]).astype(jnp.int32)
    there = [regroup_pairs(j, 16, 8, 4) for j in range(2)]
    back = [[(b, a) for a, b in pairs] for pairs in there]
    follow = follow_pairs(16, 8)
    down = [(b, b + 4) for b in range(60)]
    twin = [(h, h ^ 1) for h in range(8)]

    w, t, mark = call(
        directions_kernel, [shape((2, TOK, DH)), shape((2, TOK, TOK)), shape((8, DH), F32)], 2, flops=2**32
    )(reflect_dir, strength)
    planes = [[0, 2, 4, 6], [1, 3, 5, 7]]
    copies = pl.pallas_call(
        pieces_kernel,
        out_shape=shape((4, TOK, 256)),
        in_specs=[VMEM],
        out_specs=pl.BlockSpec(memory_space=pltpu.HBM),
        scratch_shapes=[pltpu.SemaphoreType.DMA((4,))],
        compiler_params=pltpu.CompilerParams(vmem_limit_bytes=62 * 2**20),
        cost_estimate=pl.CostEstimate(flops=0, bytes_accessed=2**20, transcendentals=0),
    )(inputs)
    gathered = lax.all_to_all(copies, "head", 0, 0, axis_index_groups=planes)
    gathered, mark = lax.optimization_barrier((gathered, mark))
    other = lax.ppermute(gathered, "head", twin)
    halves = call(halves_kernel, shape((4, 256, 256)), 2, smem=1)(at, w_out)
    other_out = lax.ppermute(halves, "head", twin)
    p0, p1, q, k, v, coef = call(
        project_kernel,
        [shape((PACK, DH)), shape((PACK, DH))] + [shape((2, TOK, DH))] * 3 + [shape((2, TOK, TOK))],
        9, smem=2, flops=2**30, late=1,
    )(at, hop_count, gathered, other, w_query, w_key, w_value, w, t, mark)
    r0 = lax.ppermute(p0, both, there[0])
    r1 = lax.ppermute(p1, both, there[1])
    acc, lse = call(
        own_kernel, [shape((2, TOK, DH), F32), shape((2, TOK, DH), F32)], 5, flops=2**31
    )(q, k, v, w, coef)
    qs, own_pair, hops = call(
        pair_kernel,
        [shape((3, 2, TOK, DH)), shape((PAIR, DH)), shape((2, 16, DH), F32)],
        3, smem=1, flops=2**28,
    )(at, r0, r1)
    d1 = lax.ppermute(own_pair, both, follow)
    d2 = lax.ppermute(own_pair, "ctx", down)
    d2, other_out = lax.optimization_barrier((d2, other_out))
    d3 = lax.ppermute(d2, both, follow)
    d4 = lax.ppermute(d2, "ctx", down)
    state = [shape((2, TOK, DH), F32)] * 3 + [shape((2, TOK, DH))]
    near = call(near_kernel, state, 5, smem=1, flops=2**31)(at, qs, hops, d1, d2)
    middle = call(middle_kernel, state, 7, smem=1, flops=2**30)(at, hops, d3, *near)
    o0, o1 = call(far_kernel, [shape((BACK, DH)), shape((BACK, DH))], 7, smem=1, flops=2**30)(
        at, hops, d4, *middle
    )
    g0 = lax.ppermute(o0, both, back[0])
    g1 = lax.ppermute(o1, both, back[1])
    mine = call(merge_kernel, shape((TOK, 2 * DH)), 5, smem=1, flops=2**28)(at, g1, g0, acc, lse)
    theirs = lax.ppermute(mine, "head", twin)
    part = call(mine_kernel, shape((4, TOK, 256), F32), 3, smem=1, flops=2**29)(at, mine, w_out)
    partial = call(output_kernel, shape((4, TOK, 256)), 3, flops=2**28)(part, theirs, other_out)
    pieces = lax.all_to_all(partial, "head", 0, 0, axis_index_groups=planes)
    return call(sum_kernel, shape((TOK, 256)), 1)(pieces)


def solution(mesh):
    placed = (
        P("ctx", "head"),
        P(None, "head"),
        P(None, "head"),
        P(None, "head"),
        P("head", None),
        P("ctx", "head"),
        P("head", "ctx"),
        P("ctx"),
    )
    return jax.shard_map(
        shards, mesh=mesh, in_specs=placed, out_specs=P("ctx", "head"), check_vma=False
    )
```

```python
import jax
import jax.numpy as jnp
from jax import lax
from jax.experimental import pallas as pl
from jax.experimental.pallas import tpu as pltpu
from jax.sharding import PartitionSpec as P

TOK = 256
DH = 128
SCALE = 1.4426950408889634 / DH**0.5
NEG = -1e30
F32 = jnp.float32
BF16 = jnp.bfloat16
HOP_ROW = 3 * TOK + DH
PACK = HOP_ROW + 16
PAIR = 4 * TOK + DH
BACK = TOK + 16
VMEM = pl.BlockSpec(memory_space=pltpu.VMEM)
SMEM = pl.BlockSpec(memory_space=pltpu.SMEM)

NN = (((1,), (0,)), ((), ()))
NT = (((1,), (1,)), ((), ()))
TN = (((0,), (0,)), ((), ()))


def dot(a, b, dims=NN):
    return lax.dot_general(a, b, dims, preferred_element_type=F32)


def split(a):
    high = a.astype(BF16)
    return high, (a - high.astype(F32)).astype(BF16)


def exact(a, b):
    (ah, al), (bh, bl) = split(a), split(b)
    return dot(ah, bh) + (dot(ah, bl) + dot(al, bh))


def call(body, outs, ins, flops=0, smem=0, late=0, scratch=()):
    return pl.pallas_call(
        body,
        out_shape=outs,
        in_specs=[SMEM] * smem + [VMEM] * (ins - smem) + [pl.BlockSpec(memory_space=pl.ANY)] * late,
        out_specs=jax.tree.map(lambda _: VMEM, outs),
        scratch_shapes=list(scratch),
        compiler_params=pltpu.CompilerParams(vmem_limit_bytes=48 * 2**20),
        cost_estimate=pl.CostEstimate(flops=flops, bytes_accessed=2**20, transcendentals=0),
    )


def lower_inverses(blocks, row, col):
    eye = (row == col).astype(F32)
    same = (row // 4) == (col // 4)
    small = [jnp.where(same, b, 0.0) for b in blocks]
    squares = [exact(s, s) for s in small]
    found = [exact(eye - s, eye + q) for s, q in zip(small, squares)]
    size = 4
    while size < DH:
        off = ((row // (2 * size)) == (col // (2 * size))) & ((row // size) != (col // size))
        left = [exact(x, jnp.where(off, b, 0.0)) for x, b in zip(found, blocks)]
        found = [x - exact(y, x) for x, y in zip(found, left)]
        size *= 2
    return found


def directions_kernel(dirs_ref, beta_ref, w_ref, t_ref, mark_ref):
    mark_ref[...] = jnp.zeros((8, DH), F32)
    row = lax.broadcasted_iota(jnp.int32, (TOK, TOK), 0)
    col = lax.broadcasted_iota(jnp.int32, (TOK, TOK), 1)
    strict = row > col
    r, c = row[:DH, :DH], col[:DH, :DH]
    dirs, lows, betas = [], [], []
    for h in range(2):
        d = dirs_ref[:, h * DH : (h + 1) * DH].astype(F32)
        d = d * lax.rsqrt(jnp.sum(d * d, axis=1, keepdims=True) + 1e-6)
        w = d.astype(BF16)
        dirs.append(w)
        beta = beta_ref[h : h + 1, :]
        column = jnp.sum(jnp.where(row == col, beta, 0.0), axis=1, keepdims=True)
        lows.append(jnp.where(strict, dot(w, w, NT) * column, 0.0))
        betas.append(beta)
    corners = []
    for low in lows:
        corners += [low[:DH, :DH], low[DH:, DH:]]
    found = lower_inverses(corners, r, c)
    for h in range(2):
        first, second = found[2 * h], found[2 * h + 1]
        cross = -exact(second, exact(lows[h][DH:, :DH], first))
        upper = jnp.concatenate([first, jnp.zeros((DH, DH), F32)], axis=1)
        lower = jnp.concatenate([cross, second], axis=1)
        t = (jnp.concatenate([upper, lower], axis=0) * betas[h]).astype(BF16)
        w_ref[h] = dirs[h]
        t_ref[h] = t


def pieces_kernel(x_ref, out_ref, held, loads, sems):
    half = TOK // 2
    rows = [pl.ds(n * half, half) for n in range(2)]
    brought = [pltpu.make_async_copy(x_ref.at[r], held.at[r], loads.at[n]) for n, r in enumerate(rows)]
    for copy in brought:
        copy.start()
    copies = []
    for n, r in enumerate(rows):
        brought[n].wait()
        for p in range(4):
            copies.append(pltpu.make_async_copy(held.at[r], out_ref.at[p, r], sems.at[n, p]))
            copies[-1].start()
    for copy in copies:
        copy.wait()


def project_kernel(
    at_ref, hop_ref, x_ref, o_ref, wq_ref, wk_ref, wv_ref, w_ref, t_ref,
    mark_ref, p0_ref, p1_ref, q_ref, k_ref, v_ref, c_ref,
):
    def product(weights):
        total = None
        for p in range(4):
            for ref, c in ((x_ref, at_ref[1]), (o_ref, 1 - at_ref[1])):
                rows = pl.ds(pl.multiple_of((2 * p + c) * 256, 256), 256)
                term = dot(ref[p], weights[rows, :])
                total = term if total is None else total + term
        return total.astype(BF16)

    del mark_ref
    query, key, value = product(wq_ref), product(wk_ref), product(wv_ref)
    for h in range(2):
        cut = slice(h * DH, (h + 1) * DH)
        q_ref[h] = query[:, cut]
        k_ref[h] = key[:, cut]
        v_ref[h] = value[:, cut]
    row = lax.broadcasted_iota(jnp.int32, (TOK, TOK), 0)
    col = lax.broadcasted_iota(jnp.int32, (TOK, TOK), 1)
    hops = hop_ref[0].astype(F32)
    eye = (row == col).astype(F32)[:DH, :DH]
    for j, p_ref in enumerate((p0_ref, p1_ref)):
        h = lax.rem(at_ref[0] + j, 2)
        q, k, w, t = q_ref[h], k_ref[h], w_ref[h], t_ref[h]
        u = dot(t, w, TN).astype(BF16)
        qdirs = jnp.where(row >= col, dot(q, w, NT), 0.0).astype(BF16)
        keydirs = jnp.where(col > row, dot(k, w, NT), 0.0).astype(BF16)
        coef = dot(qdirs, t).astype(BF16)
        c_ref[h] = coef
        qhat = q.astype(F32) - dot(coef, w)
        p_ref[0:TOK] = (qhat * SCALE).astype(BF16)
        p_ref[TOK : 2 * TOK] = (k.astype(F32) - dot(keydirs, u)).astype(BF16)
        p_ref[2 * TOK : 3 * TOK] = v_ref[h]
        p_ref[3 * TOK : HOP_ROW] = (eye - dot(u, w, TN)).astype(BF16)
        p_ref[HOP_ROW:PACK] = jnp.full((16, DH), hops, F32).astype(BF16)


def own_kernel(q_ref, k_ref, v_ref, w_ref, c_ref, acc_ref, lse_ref):
    row = lax.broadcasted_iota(jnp.int32, (TOK, TOK), 0)
    col = lax.broadcasted_iota(jnp.int32, (TOK, TOK), 1)
    for h in range(2):
        q, k, w = q_ref[h], k_ref[h], w_ref[h]
        dirkeys = jnp.where(row > col, dot(w, k, NT), 0.0).astype(BF16)
        own = (dot(q, k, NT) - dot(c_ref[h], dirkeys)) * SCALE
        own = jnp.where(row >= col, own, NEG)
        top = jnp.max(own, axis=1, keepdims=True)
        prob = jnp.exp2(own - top)
        total = jnp.sum(prob, axis=1, keepdims=True)
        acc_ref[h] = dot(prob.astype(BF16), v_ref[h]) / total
        lse_ref[h] = jnp.broadcast_to(top + jnp.log2(total), (TOK, DH))


def pair_kernel(at_ref, r0_ref, r1_ref, q_ref, pair_ref, hop_ref):
    swapped = at_ref[0] == 1

    def part(low, high):
        a, b = r0_ref[low:high], r1_ref[low:high]
        return jnp.where(swapped, b, a), jnp.where(swapped, a, b)

    q_even, q_odd = part(0, TOK)
    k_even, k_odd = part(TOK, 2 * TOK)
    v_even, v_odd = part(2 * TOK, 3 * TOK)
    a_even, a_odd = part(3 * TOK, HOP_ROW)
    h_even, h_odd = part(HOP_ROW, PACK)
    pair_ref[0:TOK] = dot(k_even, a_odd, NT).astype(BF16)
    pair_ref[TOK : 2 * TOK] = k_odd
    pair_ref[2 * TOK : 3 * TOK] = v_even
    pair_ref[3 * TOK : 4 * TOK] = v_odd
    pair_ref[4 * TOK : PAIR] = dot(a_odd, a_even).astype(BF16)
    q_ref[0, 0] = q_even
    q_ref[0, 1] = q_odd
    q_ref[1, 0] = q_even
    q_ref[1, 1] = dot(q_odd, a_even).astype(BF16)
    q_ref[2, 0] = k_even
    q_ref[2, 1] = v_even
    hop_ref[0] = h_even.astype(F32)
    hop_ref[1] = h_odd.astype(F32)


def window_step(q, keys, d, i, hops, pair):
    col = lax.broadcasted_iota(jnp.int32, (1, 2 * TOK), 1)
    distance = 2 * d + i - (col >= TOK).astype(jnp.int32)
    valid = (distance.astype(F32) <= hops) & (pair >= d)
    return dot(q, keys[0 : 2 * TOK], NT) + jnp.where(valid, 0.0, NEG)


def near_kernel(at_ref, q_ref, hop_ref, d1_ref, d2_ref, acc_ref, top_ref, total_ref, next_ref):
    pair = at_ref[2]
    for i in range(2):
        hops = hop_ref[i, 0:1, 0:1]
        q = q_ref[1, i]
        first = window_step(q, d1_ref, 1, i, hops, pair)
        q = dot(q, d1_ref[4 * TOK : PAIR]).astype(BF16)
        second = window_step(q, d2_ref, 2, i, hops, pair)
        next_ref[i] = dot(q, d2_ref[4 * TOK : PAIR]).astype(BF16)
        top = jnp.maximum(jnp.max(first, axis=1, keepdims=True), jnp.max(second, axis=1, keepdims=True))
        if i == 1:
            inside = dot(q_ref[0, 1], q_ref[2, 0], NT)
            top = jnp.maximum(top, jnp.max(inside, axis=1, keepdims=True))
        first, second = jnp.exp2(first - top), jnp.exp2(second - top)
        total = jnp.sum(first, axis=1, keepdims=True) + jnp.sum(second, axis=1, keepdims=True)
        acc = dot(first.astype(BF16), d1_ref[2 * TOK : 4 * TOK])
        acc += dot(second.astype(BF16), d2_ref[2 * TOK : 4 * TOK])
        if i == 1:
            inside = jnp.exp2(inside - top)
            total += jnp.sum(inside, axis=1, keepdims=True)
            acc += dot(inside.astype(BF16), q_ref[2, 1])
        acc_ref[i] = acc
        top_ref[i] = jnp.broadcast_to(top, (TOK, DH))
        total_ref[i] = jnp.broadcast_to(total, (TOK, DH))


def grown(q, keys, d, i, hops, pair, acc_ref, top_ref, total_ref):
    scores = window_step(q, keys, d, i, hops, pair)
    before = top_ref[i, :, 0:1]
    top = jnp.maximum(jnp.max(scores, axis=1, keepdims=True), before)
    prob = jnp.exp2(scores - top)
    kept = jnp.exp2(before - top)
    total = total_ref[i, :, 0:1] * kept + jnp.sum(prob, axis=1, keepdims=True)
    acc = acc_ref[i] * kept + dot(prob.astype(BF16), keys[2 * TOK : 4 * TOK])
    return acc, top, total


def middle_kernel(
    at_ref, hop_ref, d3_ref, acc_ref, top_ref, total_ref, q_ref, acc_out, top_out, total_out, next_ref
):
    for i in range(2):
        q, hops = q_ref[i], hop_ref[i, 0:1, 0:1]
        acc, top, total = grown(q, d3_ref, 3, i, hops, at_ref[2], acc_ref, top_ref, total_ref)
        acc_out[i] = acc
        top_out[i] = jnp.broadcast_to(top, (TOK, DH))
        total_out[i] = jnp.broadcast_to(total, (TOK, DH))
        next_ref[i] = dot(q, d3_ref[4 * TOK : PAIR]).astype(BF16)


def far_kernel(at_ref, hop_ref, d4_ref, acc_ref, top_ref, total_ref, q_ref, o0_ref, o1_ref):
    for j, out_ref in enumerate((o0_ref, o1_ref)):
        i = lax.rem(at_ref[0] + j, 2)
        hops = hop_ref[i, 0:1, 0:1]
        acc, top, total = grown(q_ref[i], d4_ref, 4, i, hops, at_ref[2], acc_ref, top_ref, total_ref)
        out_ref[0:TOK] = (acc / total).astype(BF16)
        lse = jnp.broadcast_to(top + jnp.log2(total), (TOK, DH)).T[0:16]
        high = lse.astype(BF16).astype(F32)
        low = lse - high
        line = lax.broadcasted_iota(jnp.int32, (16, DH), 0)
        tile = jnp.where(line == 0, high[:, :DH], high[:, DH:])
        tile = jnp.where(line == 2, low[:, :DH], tile)
        tile = jnp.where(line == 3, low[:, DH:], tile)
        out_ref[TOK:BACK] = tile.astype(BF16)


def merge_kernel(at_ref, g1_ref, g0_ref, acc_ref, lse_ref, out_ref):
    swapped = at_ref[0] == 1
    row = lax.broadcasted_iota(jnp.int32, (DH, DH), 0)
    col = lax.broadcasted_iota(jnp.int32, (DH, DH), 1)
    for h in range(2):
        a, b = (g0_ref, g1_ref) if h == 0 else (g1_ref, g0_ref)
        got = jnp.where(swapped, b[...], a[...]).astype(F32)
        tile = got[TOK:BACK]
        column = []
        for part in range(2):
            line = tile[part : part + 1] + tile[part + 2 : part + 3]
            column.append(jnp.sum(jnp.where(row == col, line, 0.0), axis=1, keepdims=True))
        far = jnp.concatenate(column, axis=0)
        own = lse_ref[h, :, 0:1]
        top = jnp.maximum(own, far)
        mine, theirs = jnp.exp2(own - top), jnp.exp2(far - top)
        mixed = (acc_ref[h] * mine + got[:TOK] * theirs) / (mine + theirs)
        out_ref[:, h * DH : (h + 1) * DH] = mixed.astype(BF16)


def columns(c, p):
    return pl.ds(pl.multiple_of((2 * p + c) * 256, 256), 256)


def halves_kernel(at_ref, wo_ref, out_ref):
    for p in range(4):
        out_ref[p] = wo_ref[:, columns(1 - at_ref[1], p)]


def mine_kernel(at_ref, mine_ref, wo_ref, out_ref):
    for p in range(4):
        out_ref[p] = dot(mine_ref[...], wo_ref[:, columns(at_ref[1], p)])


def output_kernel(part_ref, theirs_ref, other_ref, out_ref):
    for p in range(4):
        out_ref[p] = (part_ref[p] + dot(theirs_ref[...], other_ref[p])).astype(BF16)


def sum_kernel(x_ref, out_ref):
    total = x_ref[0].astype(F32)
    for p in range(1, 4):
        total += x_ref[p].astype(F32)
    out_ref[...] = total.astype(BF16)


def regroup_pairs(j, rows, cross, groups):
    pairs = []
    for z in range(rows):
        for x in range(4):
            for y in range(groups):
                for c in range(2):
                    i = (x + j) % 2
                    pairs.append(((z * 4 + x) * cross + y * 2 + c, (z * 4 + 2 * c + i) * cross + y * 2 + x // 2))
    return pairs


def follow_pairs(rows, cross):
    pairs = []
    for b in range(4 * rows):
        for y in range(0, cross, 2):
            pairs.append((b * cross + y, b * cross + y + 1))
            if b + 4 < 4 * rows:
                pairs.append((b * cross + y + 1, (b + 4) * cross + y))
    return pairs


def shape(dims, dtype=BF16):
    return jax.ShapeDtypeStruct(dims, dtype)


def shards(inputs, w_query, w_key, w_value, w_out, reflect_dir, strength, hop_count):
    both = ("ctx", "head")
    z = lax.axis_index("ctx") // 4
    x = lax.axis_index("ctx") % 4
    c = lax.axis_index("head") % 2
    at = jnp.stack([x % 2, c, 2 * z + c]).astype(jnp.int32)
    there = [regroup_pairs(j, 16, 8, 4) for j in range(2)]
    back = [[(b, a) for a, b in pairs] for pairs in there]
    follow = follow_pairs(16, 8)
    down = [(b, b + 4) for b in range(60)]
    twin = [(h, h ^ 1) for h in range(8)]

    w, t, mark = call(
        directions_kernel, [shape((2, TOK, DH)), shape((2, TOK, TOK)), shape((8, DH), F32)], 2, flops=2**32
    )(reflect_dir, strength)
    planes = [[0, 2, 4, 6], [1, 3, 5, 7]]
    copies = pl.pallas_call(
        pieces_kernel,
        out_shape=shape((4, TOK, 256)),
        in_specs=[pl.BlockSpec(memory_space=pltpu.HBM)],
        out_specs=pl.BlockSpec(memory_space=pltpu.HBM),
        scratch_shapes=[
            pltpu.VMEM((TOK, 256), BF16), pltpu.SemaphoreType.DMA((2,)), pltpu.SemaphoreType.DMA((2, 4)),
        ],
        compiler_params=pltpu.CompilerParams(vmem_limit_bytes=62 * 2**20),
        cost_estimate=pl.CostEstimate(flops=0, bytes_accessed=2**20, transcendentals=0),
    )(inputs)
    gathered = lax.all_to_all(copies, "head", 0, 0, axis_index_groups=planes)
    gathered, mark = lax.optimization_barrier((gathered, mark))
    other = lax.ppermute(gathered, "head", twin)
    halves = call(halves_kernel, shape((4, 256, 256)), 2, smem=1)(at, w_out)
    other_out = lax.ppermute(halves, "head", twin)
    p0, p1, q, k, v, coef = call(
        project_kernel,
        [shape((PACK, DH)), shape((PACK, DH))] + [shape((2, TOK, DH))] * 3 + [shape((2, TOK, TOK))],
        9, smem=2, flops=2**30, late=1,
    )(at, hop_count, gathered, other, w_query, w_key, w_value, w, t, mark)
    r0 = lax.ppermute(p0, both, there[0])
    r1 = lax.ppermute(p1, both, there[1])
    acc, lse = call(
        own_kernel, [shape((2, TOK, DH), F32), shape((2, TOK, DH), F32)], 5, flops=2**31
    )(q, k, v, w, coef)
    qs, own_pair, hops = call(
        pair_kernel,
        [shape((3, 2, TOK, DH)), shape((PAIR, DH)), shape((2, 16, DH), F32)],
        3, smem=1, flops=2**28,
    )(at, r0, r1)
    d1 = lax.ppermute(own_pair, both, follow)
    d2 = lax.ppermute(own_pair, "ctx", down)
    d2, other_out = lax.optimization_barrier((d2, other_out))
    d3 = lax.ppermute(d2, both, follow)
    d4 = lax.ppermute(d2, "ctx", down)
    state = [shape((2, TOK, DH), F32)] * 3 + [shape((2, TOK, DH))]
    near = call(near_kernel, state, 5, smem=1, flops=2**31)(at, qs, hops, d1, d2)
    middle = call(middle_kernel, state, 7, smem=1, flops=2**30)(at, hops, d3, *near)
    o0, o1 = call(far_kernel, [shape((BACK, DH)), shape((BACK, DH))], 7, smem=1, flops=2**30)(
        at, hops, d4, *middle
    )
    g0 = lax.ppermute(o0, both, back[0])
    g1 = lax.ppermute(o1, both, back[1])
    mine = call(merge_kernel, shape((TOK, 2 * DH)), 5, smem=1, flops=2**28)(at, g1, g0, acc, lse)
    theirs = lax.ppermute(mine, "head", twin)
    part = call(mine_kernel, shape((4, TOK, 256), F32), 3, smem=1, flops=2**29)(at, mine, w_out)
    partial = call(output_kernel, shape((4, TOK, 256)), 3, flops=2**28)(part, theirs, other_out)
    pieces = lax.all_to_all(partial, "head", 0, 0, axis_index_groups=planes)
    return call(sum_kernel, shape((TOK, 256)), 1)(pieces)


def solution(mesh):
    placed = (
        P("ctx", "head"),
        P(None, "head"),
        P(None, "head"),
        P(None, "head"),
        P("head", None),
        P("ctx", "head"),
        P("head", "ctx"),
        P("ctx"),
    )
    return jax.shard_map(
        shards, mesh=mesh, in_specs=placed, out_specs=P("ctx", "head"), check_vma=False
    )
```
